32 devices in a mesh: day: 4 (over y, x), tile: 8 (over z, core).
Axes of the slice: x: 2, y: 2, z: 4, core: 2. Of those that a mesh axis runs over, the one named last changes fastest.
Arguments:
- scene_rows: bfloat16 [4, 4, 8, 512, 128], P(None, 'day', 'tile'), may hold values from -6 to 6
- granule_list: int32 [32, 8, 4, 3], P('day', 'tile'), may hold values from 0 to 16, as said below
- land_mask: int32 [64, 1024], P('day', 'tile'), may hold values 0 or 1
- in_weight: bfloat16 [16, 4], replicated, may hold values from -3 to 3
- obs_bias: float32 [16], replicated, may hold values from -3 to 3
- time_taps: float32 [4, 16, 3], replicated, may hold values from -3 to 3
- mix_weight: bfloat16 [4, 16, 16], replicated, may hold values from -1.5 to 1.5
- mix_bias: float32 [4, 16], replicated, may hold values from -3 to 3
- space_taps: float32 [4, 16, 9], replicated, may hold values from -2.5 to 2.5
- out_weight: bfloat16 [16], replicated, may hold values from -1.5 to 1.5
- out_bias: float32 [1], replicated, may hold values from -3 to 3
Outputs:
- filled: float32 [32, 64, 1024], P(None, 'day', 'tile')
The draws below stay inside these ranges and needn't reach their ends.
Inputs may be any that keep to these rules, and one draw needn't show every extreme that they name: `granule_list`: on each day and band the 8 owners of a day group name every tile once; one owner names one tile for one band on at most 1 days; offset + count <= 16; on each band some tile has count 16 on every day.
All inputs are finite; a program needn't handle non-finite values. No bound on the sum of `land_mask` on one device may be relied on, other than what follows from the above.
Results may differ from the reference program's by a relative error of at most 0.011.
Values may be sent and summed in bfloat16 or wider, within the bound.
No kernel may reach another device: no remote copies, remote signals or barrier semaphores. Data moves between devices by JAX's collectives and lax.ppermute only.
A program may use at most 64 MiB of HBM per device.

```python
import jax
import jax.numpy as jnp
from jax import lax

CH = 16
VARS = 4
COLS = 128
LAYERS = 4
DAY_DEV = 8
ROWS = 16
DAYS = 32
NR = 64
NC = 1024
PACK = 512
N_DAY = 4
N_TILE = 8


def draw_granule_list(key, part):
    base = jax.random.fold_in(key, 7)
    key_perm, key_level, key_clear, key_count, key_offset = jax.random.split(base, 5)
    span_len = max(N_TILE, DAY_DEV)
    perm_keys = jax.random.split(key_perm, N_DAY * N_DAY)
    orders = jax.vmap(lambda one_key: jax.random.permutation(one_key, span_len))(perm_keys)
    shifts = (orders[:, :DAY_DEV] % N_TILE).reshape(N_DAY, N_DAY, DAY_DEV)
    shifts = jnp.transpose(shifts, (0, 2, 1)).reshape(DAYS, N_DAY)
    senders = jnp.arange(N_TILE, dtype=jnp.int32)
    tile_ids = ((senders[None, :, None] + shifts[:, None, :]) % N_TILE).astype(jnp.int32)
    levels = jax.random.randint(key_level, (N_DAY, N_TILE), ROWS // 4, ROWS + 1)
    clear_tile = jax.random.randint(key_clear, (N_DAY,), 0, N_TILE)
    levels = jnp.where(senders[None, :] == clear_tile[:, None], ROWS, levels)
    band_ids = jnp.broadcast_to(jnp.arange(N_DAY, dtype=jnp.int32)[None, None, :], tile_ids.shape)
    level_here = levels[band_ids, tile_ids]
    is_full = tile_ids == clear_tile[None, None, :]
    counts = jax.random.randint(key_count, tile_ids.shape, level_here // 2, level_here + 1)
    counts = jnp.where(is_full, ROWS, counts)
    offsets = jax.random.randint(key_offset, tile_ids.shape, 0, ROWS - counts + 1)
    return jnp.stack([tile_ids, offsets, counts], axis=-1).astype(jnp.int32)


def with_ends(drawn, key, smallest, high):
    index_at = [jax.random.randint(jax.random.fold_in(key, axis), (), 0, length) for axis, length in enumerate(drawn.shape)]
    main_axis = drawn.shape.index(max(drawn.shape))
    beside = index_at[:main_axis] + [(index_at[main_axis] + 1) % drawn.shape[main_axis]] + index_at[main_axis + 1:]
    return drawn.at[tuple(index_at)].set(smallest).at[tuple(beside)].set(high)


def steps_of(rng, shape, cuts, least, largest):
    factor_of, own = 1.0, jax.random.fold_in(rng, 6)
    for axis_at, blocks in cuts:
        draws = jnp.exp(jax.random.uniform(jax.random.fold_in(own, axis_at), (blocks,), jnp.float32, least / len(cuts), largest / len(cuts)))
        factor_of = factor_of * jnp.repeat(draws, shape[axis_at] // blocks).reshape([-1 if axis == axis_at else 1 for axis in range(len(shape))])
    return factor_of


def centred(stream_key, dims, deviation, limit, pieces=(), held_as=jnp.bfloat16):
    drawn = jax.random.normal(stream_key, dims, jnp.float32) * deviation
    if len(pieces) > 0:
        drawn = steps_of(stream_key, dims, pieces, -0.22, 0.18) * drawn
    return jnp.clip(drawn, min=-limit, max=limit).astype(held_as)


def setup_inputs(seed: int = 0) -> dict:
    streams_of = jax.random.split(jax.random.key(seed), 12)
    return {
        "scene_rows": centred(streams_of[0], (VARS, N_DAY, N_TILE, PACK, COLS), 1.0, 6.0, ((1, 4), (2, 8))),
        "granule_list": draw_granule_list(jax.random.fold_in(streams_of[11], 71), 0),
        "land_mask": with_ends((jax.random.randint(streams_of[2], (NR, NC), 0, 5) < 4).astype(jnp.int32), jax.random.fold_in(streams_of[2], 1), 0, 1),
        "in_weight": centred(streams_of[3], (CH, VARS), VARS ** -0.5, 3.0),
        "obs_bias": centred(streams_of[4], (CH,), 0.5, 3.0, (), jnp.float32),
        "time_taps": centred(streams_of[5], (LAYERS, CH, 3), 0.5, 3.0, (), jnp.float32),
        "mix_weight": centred(streams_of[6], (LAYERS, CH, CH), CH ** -0.5, 1.5),
        "mix_bias": centred(streams_of[7], (LAYERS, CH), 0.5, 3.0, (), jnp.float32),
        "space_taps": centred(streams_of[8], (LAYERS, CH, 9), 0.35, 2.5, (), jnp.float32),
        "out_weight": centred(streams_of[9], (CH,), CH ** -0.5, 1.5),
        "out_bias": centred(streams_of[10], (1,), 1.0, 3.0, (), jnp.float32),
    }


def place_scenes(scene_rows, granule_list):
    entries = jnp.transpose(granule_list.reshape(N_DAY, DAY_DEV, N_TILE, N_DAY, 3), (0, 2, 1, 3, 4))
    tile_ids = entries[..., 0]
    row_start = entries[..., 1]
    row_span = entries[..., 2]
    flat_counts = row_span.reshape(N_DAY, N_TILE, DAY_DEV * N_DAY)
    pack_start = (jnp.cumsum(flat_counts, axis=2, dtype=jnp.int32) - flat_counts).reshape(row_span.shape)
    row_ids = jnp.arange(ROWS, dtype=jnp.int32)
    is_live = (row_ids >= row_start[..., None]) & (row_ids < (row_start + row_span)[..., None])
    position = jnp.clip(pack_start[..., None] + row_ids - row_start[..., None], 0, PACK - 1)
    owners = jnp.arange(N_DAY, dtype=jnp.int32)[:, None] * N_TILE + jnp.arange(N_TILE, dtype=jnp.int32)[None, :]
    flat_index = (owners[:, :, None, None, None] * PACK + position).reshape(-1).astype(jnp.int32)
    packed = scene_rows.reshape(VARS, N_DAY * N_TILE * PACK, COLS)
    picked = jnp.take(packed, flat_index, axis=1).reshape(VARS, N_DAY, N_TILE, DAY_DEV, N_DAY, ROWS, COLS)
    picked = jnp.transpose(picked, (1, 2, 3, 4, 0, 5, 6))
    day_index = jnp.arange(N_DAY, dtype=jnp.int32)[:, None, None, None] * DAY_DEV + jnp.arange(DAY_DEV, dtype=jnp.int32)[None, None, :, None]
    day_index = jnp.broadcast_to(day_index, tile_ids.shape).astype(jnp.int32)
    band_index = jnp.broadcast_to(jnp.arange(N_DAY, dtype=jnp.int32)[None, None, None, :], tile_ids.shape).astype(jnp.int32)
    grid_rows = jnp.zeros((DAYS, N_DAY, N_TILE, VARS, ROWS, COLS), scene_rows.dtype)
    grid_rows = grid_rows.at[day_index, band_index, tile_ids].set(picked)
    covered = jnp.zeros((DAYS, N_DAY, N_TILE, ROWS), jnp.float32)
    covered = covered.at[day_index, band_index, tile_ids].set(is_live.astype(jnp.float32))
    observed = jnp.transpose(grid_rows, (3, 0, 1, 4, 2, 5)).reshape(VARS, DAYS, NR, NC)
    covered = jnp.transpose(covered, (0, 1, 3, 2)).reshape(DAYS, NR, N_TILE)
    return observed, covered


def reference(scene_rows, granule_list, land_mask, in_weight, obs_bias, time_taps, mix_weight, mix_bias, space_taps, out_weight, out_bias):
    observed, covered = place_scenes(scene_rows, granule_list)
    land_float = land_mask.astype(jnp.float32)
    highest = lax.Precision.HIGHEST

    def stem_column(column, current):
        start_col = (column * COLS).astype(jnp.int32)
        obs_block = lax.dynamic_slice_in_dim(observed, start_col, COLS, 3).astype(jnp.float32)
        land_block = lax.dynamic_slice_in_dim(land_float, start_col, COLS, 1)
        seen_block = lax.dynamic_slice_in_dim(covered, column.astype(jnp.int32), 1, 2)
        stem_out = jnp.einsum("cv,vdrq->cdrq", in_weight.astype(jnp.float32), obs_block, precision=highest) + obs_bias[:, None, None, None]
        keep_mask = (seen_block * land_block[None]).astype(jnp.bfloat16)
        col_block = stem_out.astype(jnp.bfloat16) * keep_mask[None]
        return lax.dynamic_update_slice_in_dim(current, col_block, start_col, 3)

    current = lax.fori_loop(0, N_TILE, stem_column, jnp.zeros((CH, DAYS, NR, NC), jnp.bfloat16))
    for block_id in range(LAYERS):
        spacing = 2 ** block_id
        tap_set = time_taps[block_id][:, :, None, None, None]
        mix_now = mix_weight[block_id].astype(jnp.float32)
        bias_now = mix_bias[block_id]
        space_now = space_taps[block_id]

        def mix_column(column, spread):
            start_col = (column * COLS).astype(jnp.int32)
            col_block = lax.dynamic_slice_in_dim(current, start_col, COLS, 3).astype(jnp.float32)
            padded = jnp.pad(col_block, ((0, 0), (spacing, spacing), (0, 0), (0, 0)))
            mixed_in = tap_set[:, 0] * padded[:, :DAYS] + tap_set[:, 1] * col_block + tap_set[:, 2] * padded[:, 2 * spacing:2 * spacing + DAYS]
            mixed_in = lax.optimization_barrier(mixed_in.astype(jnp.bfloat16))
            mixed_out = jnp.einsum("oc,cdrq->odrq", mix_now, mixed_in.astype(jnp.float32), precision=highest) + bias_now[:, None, None, None]
            return lax.dynamic_update_slice_in_dim(spread, jax.nn.silu(mixed_out).astype(jnp.bfloat16), start_col, 3)

        spread = lax.fori_loop(0, N_TILE, mix_column, jnp.zeros((CH, DAYS, NR, NC), jnp.bfloat16))

        def space_channel(channel, current):
            x_chan = lax.dynamic_index_in_dim(current, channel, 0, keepdims=False).astype(jnp.float32)
            v_chan = lax.dynamic_index_in_dim(spread, channel, 0, keepdims=False).astype(jnp.float32)
            weights = lax.dynamic_index_in_dim(space_now, channel, 0, keepdims=False)
            padded = jnp.pad(v_chan, ((0, 0), (1, 1), (1, 1)))
            running = x_chan
            for row_off in range(3):
                for col_off in range(3):
                    running = running + weights[3 * row_off + col_off] * padded[:, row_off:row_off + NR, col_off:col_off + NC]
            return lax.dynamic_update_index_in_dim(current, running.astype(jnp.bfloat16), channel, 0)

        current = lax.fori_loop(0, CH, space_channel, current)

    def out_column(column, filled):
        start_col = (column * COLS).astype(jnp.int32)
        col_block = lax.dynamic_slice_in_dim(current, start_col, COLS, 3).astype(jnp.float32)
        result = jnp.einsum("c,cdrq->drq", out_weight.astype(jnp.float32), col_block, precision=highest) + out_bias[0]
        land_block = lax.dynamic_slice_in_dim(land_float, start_col, COLS, 1)
        return lax.dynamic_update_slice_in_dim(filled, result * land_block[None], start_col, 2)

    return lax.fori_loop(0, N_TILE, out_column, jnp.zeros((DAYS, NR, NC), jnp.float32))
```

```python
import functools

import jax
import jax.numpy as jnp
from jax import lax
from jax.experimental import pallas as pl
from jax.experimental.pallas import tpu as pltpu
from jax.sharding import PartitionSpec as P

BF = jnp.bfloat16
F32 = jnp.float32
HALO = 4
LANES = 128
VMEM = pl.BlockSpec(memory_space=pltpu.VMEM)
SMEM = pl.BlockSpec(memory_space=pltpu.SMEM)
ANY = pl.BlockSpec(memory_space=pl.ANY)


def iota(shape, dim):
    return lax.broadcasted_iota(jnp.int32, shape, dim)


def pack_kernel(tiles, bands, days, scene_ref, list_ref, out_ref, wide, mixed, blocks, picked, tail):
    variables, slots = scene_ref.shape[0], scene_ref.shape[1]

    def clear(i, c):
        out_ref[i] = jnp.zeros(out_ref.shape[1:], BF)
        return c

    lax.fori_loop(0, out_ref.shape[0], clear, 0)

    def clear_tail(i, c):
        tail[i] = jnp.zeros((8, LANES), F32)
        return c

    lax.fori_loop(0, tail.shape[0], clear_tail, 0)
    for v in range(variables):
        wide[v, 0:16] = jnp.zeros((16, LANES), F32)
        wide[v, 16 : 16 + slots] = scene_ref[v].astype(F32)
        wide[v, 16 + slots : 32 + slots] = jnp.zeros((16, LANES), F32)
    row = iota((16, LANES), 0)

    def place(day, first):
        for band in range(bands):
            base = (day * bands + band) * 3
            tile, offset, count = list_ref[base], list_ref[base + 1], list_ref[base + 2]
            live = (row >= offset) & (row < offset + count)
            for v in range(variables):
                rows = wide[v, pl.ds(16 + first - offset, 16), :]
                mixed[band, pl.ds(v, 16, stride=4), :] = jnp.where(live, rows, 0.0)
            block = mixed[band].astype(BF)
            blocks[day * bands + band] = block
            out_ref[band * tiles + tile, 16:80] = block
            if band + 1 < bands:
                out_ref[(band + 1) * tiles + tile, 0:16] = block[48:64]
            if band > 0:
                out_ref[(band - 1) * tiles + tile, 80:96] = block[0:16]
            first = first + count
        return first

    lax.fori_loop(0, days, place, jnp.int32(0))

    q, lane = iota((LANES, LANES), 0), iota((LANES, LANES), 1)
    edge = lane % 8
    choose = (q == jnp.where(edge < 4, 124 + edge, edge - 4)).astype(F32).astype(BF)
    granules = days * bands
    spread = jnp.dot(
        blocks[...].reshape(granules * 64, LANES), choose, preferred_element_type=F32
    ).reshape(granules, 64, LANES)
    r64, l64 = iota((64, LANES), 0), iota((64, LANES), 1)
    own = (r64 % 4 == l64 // 32) & ((r64 // 4) % 4 == (l64 % 32) // 8)
    for g in range(granules):
        kept = jnp.where(own, spread[g], 0.0)
        part = [jnp.sum(kept[16 * j : 16 * j + 16], axis=0, keepdims=True) for j in range(4)]
        zero = jnp.zeros((2, LANES), F32)
        picked[g] = jnp.concatenate([part[3], part[0], part[1], part[2], part[3], part[0], zero], 0)

    sub, col = iota((8, LANES), 0), iota((8, LANES), 1)
    row_of = {0: (sub >= 1) & (sub <= 4), 1: sub == 0, -1: sub == 5}
    is_left = col % 8 < 4
    day_base = list_ref[days * bands * 3] * days

    def tags(day, c):
        for band in range(bands):
            base = (day * bands + band) * 3
            tile, offset, count = list_ref[base], list_ref[base + 1], list_ref[base + 2]
            sides = picked[day * bands + band]
            for step, shift, low, high, region in ((0, 4, 0, 16, 1), (1, -12, 12, 16, 0), (-1, 20, 0, 4, 2)):
                lo, hi = jnp.maximum(offset, low), jnp.minimum(offset + count, high)
                for side in range(3):
                    r = col - (24 * side + shift)
                    tag = jnp.where(col == 72 + 3 * side + region, (day_base + day + 1).astype(F32), 0.0)
                    note = jnp.where(sub == 6, jnp.where((r >= lo) & (r < hi), 1.0, tag), 0.0)
                    if side > 0:
                        wanted = row_of[step] & (is_left if side == 1 else jnp.logical_not(is_left))
                        note = note + jnp.where(wanted, sides, 0.0)
                    at = (band + step + 1) * (tiles + 2) + tile + (1, 2, 0)[side]
                    tail[at] = tail[at] + note
        return c

    lax.fori_loop(0, days, tags, 0)
    for band in range(bands):

        def finish(tile, c, band=band):
            out_ref[band * tiles + tile, 96:104] = tail[(band + 1) * (tiles + 2) + tile + 1].astype(BF)
            return c

        lax.fori_loop(0, tiles, finish, 0)


def banded_kernel(width, taps_ref, out_ref):
    at = pl.program_id(0)
    taps = [taps_ref[at * 9 + k] for k in range(9)]
    delta = [(k // 3 - 1) * width + k % 3 - 1 for k in range(9)]
    offset = iota((16, LANES), 0) - iota((16, LANES), 1)
    for k0 in range(0, 768, 16):
        for n0 in range(0, 256, LANES):
            value = jnp.zeros((16, LANES), F32)
            for tap, d in zip(taps, delta):
                want = d + 256 - k0 + n0
                if -(LANES - 1) <= want <= 15:
                    value = jnp.where(offset == want, tap, value)
            out_ref[0, k0 : k0 + 16, n0 : n0 + LANES] = value.astype(BF)


def chunked(low, high, step, fn):
    count = (high - low) // step
    spare = (high - low) - count * step
    for i in range(low, low + spare):
        fn(i)

    def body(i, c):
        for u in range(step):
            fn(low + spare + i * step + u)
        return c

    lax.fori_loop(0, count, body, 0)


def main_kernel(
    sources,
    arrived_ref,
    land_ref,
    valid_ref,
    own_land_ref,
    expand_ref,
    in_ref,
    first_ref,
    rest_ref,
    bias_ref,
    out_w_ref,
    out_b_ref,
    banded_ref,
    out_ref,
    x_ref,
    v_ref,
    taps,
    y_ref,
    sem,
):
    channels = banded_ref.shape[1]
    layers = banded_ref.shape[0]
    width = LANES + 2 * HALO
    rows_in = 24

    def fetch(l):
        return pltpu.make_async_copy(banded_ref.at[l], taps.at[l % 2], sem.at[l % 2])

    fetch(0).start()
    fetch(1).start()

    tail = arrived_ref[:, 96:104, :].astype(F32).reshape(8 * sources, LANES).astype(BF)
    pick_r, pick_c = iota((7 * sources, 8 * sources), 0), iota((7 * sources, 8 * sources), 1)
    pick = ((pick_c // 8 == pick_r % sources) & (pick_c % 8 == pick_r // sources)).astype(F32).astype(BF)
    parts = jnp.dot(pick, tail, preferred_element_type=F32).astype(BF)
    side_rows = [parts[j * sources : (j + 1) * sources] for j in range(6)]
    meta = parts[6 * sources :]
    wanted = (iota((16, LANES), 1) == iota((16, LANES), 0) + 72).astype(F32).astype(BF)
    tag_rows = lax.dot_general(wanted, meta, (((1,), (1,)), ((), ())), preferred_element_type=F32)
    repeat = (iota((sources, 8 * sources), 1) // 8 == iota((sources, 8 * sources), 0)).astype(F32).astype(BF)
    tag_wide = jnp.dot(tag_rows.astype(BF), repeat, preferred_element_type=F32)
    m, k = iota((256, 8 * sources), 0), iota((256, 8 * sources), 1)
    same = m // 32 == k % 8
    day_of = (m % 32 + 1).astype(F32)
    perms = [
        jnp.where(same & (tag_wide[b : b + 1] == day_of), 1.0, 0.0).astype(BF) for b in range(3)
    ]
    day_col = (iota((32, sources), 0) + 1).astype(F32)
    hot = [jnp.where(tag_rows[i : i + 1] == day_col, 1.0, 0.0).astype(BF) for i in range(9)]

    lane32 = iota((32, LANES), 1)
    cover = jnp.zeros((32, LANES), F32)
    for side in range(3):
        for band, (lo, hi) in enumerate(((0, 4), (4, 20), (20, 24))):
            got = jnp.dot(hot[3 * side + band], meta, preferred_element_type=F32)
            here = (lane32 >= 24 * side + lo) & (lane32 < 24 * side + hi)
            cover = jnp.where(here, got, cover)
    cover = cover.astype(BF)

    packed = [[None] * 2 for _ in range(4)]
    for j in range(6):
        band = 0 if j == 0 else (2 if j == 5 else 1)
        left = jnp.dot(hot[3 + band], side_rows[j], preferred_element_type=F32)
        right = jnp.dot(hot[6 + band], side_rows[j], preferred_element_type=F32)
        both = jnp.where(lane32 % 8 < 4, left, right)
        half, start = (32 * j) // LANES, (32 * j) % LANES
        here = (lane32 >= start) & (lane32 < start + 32)
        for v in range(4):
            moved = pltpu.roll(both, (start - 32 * v) % LANES, 1)
            had = packed[v][half]
            packed[v][half] = jnp.where(here, moved, 0.0 if had is None else had)
    edges = [jnp.concatenate([packed[v][h] for v in range(4)], 0) for h in range(2)]

    rolled = []
    for p in range(12):
        band = 0 if p < 2 else (2 if p >= 10 else 1)
        rows = arrived_ref[:, 8 * p : 8 * p + 8, :].astype(F32).reshape(8 * sources, LANES).astype(BF)
        got = jnp.dot(perms[band], rows, preferred_element_type=F32)
        for r2 in range(2):
            row = 2 * p + r2
            rolled.append(pltpu.roll(got[128 * r2 : 128 * r2 + 128], (8 * row + 4) % LANES, 1))
    lane = iota((LANES, LANES), 1)
    zero = jnp.zeros((LANES, LANES), F32)

    def flat_block(b):
        now, start = (b, 8 * b + 4) if b <= 15 else ((b - 1, 8 * b - 132) if b >= 17 else (16, 132))
        before = now - 1
        now_v = rolled[now] if now < rows_in else zero
        before_v = rolled[before] if before >= 0 else zero
        edge = edges[0] if b <= 16 else edges[1]
        return jnp.where(lane < start - 8, before_v, jnp.where(lane < start, edge, now_v))

    for j in range(13):
        pair = []
        for b in (2 * j, 2 * j + 1):
            keep = jnp.dot(cover, expand_ref[b], preferred_element_type=F32)
            pair.append((jnp.concatenate([flat_block(b), keep, keep], 0) * land_ref[b : b + 1]).astype(BF))
        got = jnp.dot(in_ref[...], jnp.concatenate(pair, 1), preferred_element_type=F32).astype(BF)
        x_ref[2 * j] = got[:, :LANES]
        x_ref[2 * j + 1] = got[:, LANES:]

    for b in (0, 1, 28, 29):
        v_ref[b] = jnp.zeros(v_ref.shape[1:], BF)

    def mix(l, j):
        both = jnp.concatenate([x_ref[2 * j], x_ref[2 * j + 1]], 1)
        ok = jnp.concatenate([valid_ref[pl.ds(2 * j, 1)], valid_ref[pl.ds(2 * j + 1, 1)]], 1)
        bias = bias_ref[l]
        for p in range(2):
            half = slice(256 * p, 256 * p + 256)
            if l == 0:
                acc = jnp.dot(first_ref[half], both, preferred_element_type=F32)
            else:
                acc = jnp.dot(rest_ref[l - 1, p], both[half], preferred_element_type=F32)
            h = acc + jnp.concatenate([bias[half], bias[half]], 1)
            v = ((h + h * jnp.tanh(h)) * ok).astype(BF)
            v_ref[2 * j + 2, half] = v[:, :LANES]
            v_ref[2 * j + 3, half] = v[:, LANES:]

    def stencil(l, low, high, c):
        groups = [pl.ds(pl.multiple_of(c * 16 + 256 * p, 16), 16) for p in range(2)]
        lhs = jnp.concatenate(
            [
                jnp.concatenate([v_ref[2 * j + b, rows] for b in range(6)], 1)
                for j in range(low, high)
                for rows in groups
            ],
            0,
        )
        acc = jnp.dot(lhs, taps[l % 2, c], preferred_element_type=F32)
        at = 0
        for j in range(low, high):
            for rows in groups:
                for h in range(2):
                    part = acc[at : at + 16, LANES * h : LANES * h + LANES]
                    x_ref[2 * j + h, rows] = (x_ref[2 * j + h, rows].astype(F32) + part).astype(BF)
                at += 16

    for l in range(layers):
        low_v, high_v = l * width // 256, -(-(rows_in - l) * width // 256)
        low_x, high_x = (l + 1) * width // 256, -(-(rows_in - l - 1) * width // 256)
        chunked(low_v, high_v, 4, functools.partial(mix, l))
        fetch(l).wait()
        chunked(0, channels, 4, functools.partial(stencil, l, low_x, high_x))
        if l + 2 < layers:
            fetch(l + 2).start()

    for j in range(2, 11):
        got = jnp.dot(
            out_w_ref[...], jnp.concatenate([x_ref[2 * j], x_ref[2 * j + 1]], 1), preferred_element_type=F32
        )
        y_ref[2 * j] = got[:, :LANES]
        y_ref[2 * j + 1] = got[:, LANES:]
    lane_d = iota((32, LANES), 1)
    for r in range(16):
        block, start = divmod((r + HALO) * width + HALO, LANES)
        back = (LANES - start) % LANES
        value = pltpu.roll(y_ref[block], back, 1) if back else y_ref[block]
        if start:
            value = jnp.where(lane_d < LANES - start, value, pltpu.roll(y_ref[block + 1], back, 1))
        out_ref[:, r, :] = (value + out_b_ref[0]) * own_land_ref[r : r + 1]


def local(
    scene_rows,
    granule_list,
    land_mask,
    in_weight,
    obs_bias,
    time_taps,
    mix_weight,
    mix_bias,
    space_taps,
    out_weight,
    out_bias,
):
    bands = lax.axis_size("day")
    tiles = lax.axis_size("tile")
    days_here = granule_list.shape[0]
    days = days_here * bands
    rows, cols = land_mask.shape
    channels, variables = in_weight.shape
    layers = mix_weight.shape[0]
    sources = bands * tiles
    width = cols + 2 * HALO
    tall = rows + 2 * HALO
    band_at, tile_at = lax.axis_index("day"), lax.axis_index("tile")
    slots = scene_rows.shape[3]
    n_block = 26

    notes = jnp.concatenate([granule_list.reshape(-1), band_at.reshape(1).astype(jnp.int32)])
    granules = days_here * bands
    outgoing = pl.pallas_call(
        functools.partial(pack_kernel, tiles, bands, days_here),
        out_shape=jax.ShapeDtypeStruct((sources, 104, cols), BF),
        in_specs=[VMEM, SMEM],
        out_specs=VMEM,
        scratch_shapes=[
            pltpu.VMEM((variables, slots + 32, cols), F32),
            pltpu.VMEM((bands, 64, cols), F32),
            pltpu.VMEM((granules, 64, cols), BF),
            pltpu.VMEM((granules, 8, cols), F32),
            pltpu.VMEM(((bands + 2) * (tiles + 2), 8, cols), F32),
        ],
        compiler_params=pltpu.CompilerParams(vmem_limit_bytes=32 * 2**20),
        name="pack",
    )(scene_rows.reshape(variables, slots, cols), notes)
    arrived = lax.all_to_all(outgoing, ("day", "tile"), split_axis=0, concat_axis=0, tiled=True)

    half = days // 2
    order = jnp.arange(2 * channels * half)
    ch_of = (order // half) % channels
    day_of = 2 * (order % half) + order // (channels * half)
    gap = day_of[None, :] - day_of[:, None]
    pair = [mix_weight[l].astype(F32)[ch_of][:, ch_of] for l in range(0)]
    del pair

    def day_matrix(l, n_par):
        spacing = 2**l
        w = 0.5 * mix_weight[l].astype(F32)[:, :, None] * time_taps[l][None, :, :]
        d = 2 * jnp.arange(half)[None, :] + jnp.arange(2)[:, None]
        diff = d[None, None, :, :] - d[:, :, None, None]
        hit = jnp.stack([(diff == (k - 1) * spacing).astype(F32) for k in range(3)], -1)
        full = sum(
            w[None, :, None, None, :, None, k] * hit[:, None, :, :, None, :, k] for k in range(3)
        )
        return full.astype(BF)

    first = day_matrix(0, 2).reshape(channels * days, channels * days)
    rest = jnp.stack(
        [
            jnp.stack(
                [
                    day_matrix(l, 2)[p, :, :, p].reshape(channels * half, channels * half)
                    for p in range(2)
                ]
            )
            for l in range(1, layers)
        ]
    )
    by_row = lambda a: jnp.broadcast_to(a[..., None, :, None], a.shape[:-1] + (2, channels, half)).reshape(
        a.shape[:-1] + (channels * days,)
    )
    bias = jnp.broadcast_to(0.5 * by_row(mix_bias)[..., None], (layers, channels * days, LANES))
    same_day = (day_of[:, None] == jnp.arange(days)[None, :]).astype(F32)
    bias_hi = obs_bias.astype(BF).astype(F32)
    in_cols = [by_row(in_weight[:, v].astype(F32))[:, None] * same_day for v in range(variables)]
    in_cols += [by_row(b)[:, None] * same_day for b in (bias_hi, obs_bias - bias_hi)]
    in_full = jnp.concatenate(in_cols, 1).astype(BF)
    out_full = (by_row(out_weight.astype(F32))[:, None] * same_day).T.astype(BF)

    banded = pl.pallas_call(
        functools.partial(banded_kernel, width),
        grid=(layers * channels,),
        out_shape=jax.ShapeDtypeStruct((layers * channels, 768, 256), BF),
        in_specs=[SMEM],
        out_specs=pl.BlockSpec((1, 768, 256), lambda i: (i, 0, 0)),
        cost_estimate=pl.CostEstimate(
            flops=64 * 768 * 256 * 8, bytes_accessed=64 * 768 * 256 * 2, transcendentals=0
        ),
        name="banded",
    )(space_taps.reshape(-1)).reshape(layers, channels, 768, 256)

    forward = lambda n: [(i, i + 1) for i in range(n - 1)]
    backward = lambda n: [(i + 1, i) for i in range(n - 1)]
    land = land_mask.astype(BF)
    land = jnp.concatenate(
        [
            lax.ppermute(land[rows - HALO :], "day", forward(bands)),
            land,
            lax.ppermute(land[:HALO], "day", backward(bands)),
        ],
        0,
    )
    land = jnp.concatenate(
        [
            lax.ppermute(land[:, cols - HALO :], "tile", forward(tiles)),
            land,
            lax.ppermute(land[:, :HALO], "tile", backward(tiles)),
        ],
        1,
    ).astype(F32)
    r, q = jnp.arange(tall)[:, None], jnp.arange(width)[None, :]
    outside = ((r < HALO) & (band_at == 0)) | ((r >= rows + HALO) & (band_at == bands - 1))
    outside = outside | ((q < HALO) & (tile_at == 0)) | ((q >= cols + HALO) & (tile_at == tiles - 1))
    valid = jnp.where(outside, 0.0, 1.0)
    flat = lambda a: jnp.pad(a.reshape(-1), (0, n_block * LANES - tall * width)).reshape(n_block, LANES)
    position = jnp.arange(n_block * LANES).reshape(n_block, 1, LANES)
    region = jnp.where(position % width < HALO, 1, jnp.where(position % width >= cols + HALO, 2, 0))
    slot = jnp.where(position < tall * width, 24 * region + position // width, -1)
    expand = (slot == jnp.arange(LANES)[None, :, None]).astype(BF)

    return pl.pallas_call(
        functools.partial(main_kernel, sources),
        out_shape=jax.ShapeDtypeStruct((days, rows, cols), F32),
        in_specs=[VMEM] * 10 + [SMEM, ANY],
        out_specs=VMEM,
        scratch_shapes=[
            pltpu.VMEM((n_block, channels * days, LANES), BF),
            pltpu.VMEM((n_block + 4, channels * days, LANES), BF),
            pltpu.VMEM((2, channels, 768, 256), BF),
            pltpu.VMEM((n_block, days, LANES), F32),
            pltpu.SemaphoreType.DMA((2,)),
        ],
        compiler_params=pltpu.CompilerParams(vmem_limit_bytes=44 * 2**20),
        name="blocks",
    )(
        arrived,
        flat(land),
        flat(valid),
        land_mask.astype(F32),
        expand,
        in_full,
        first,
        rest,
        bias,
        out_full,
        out_bias,
        banded,
    )


def solution(mesh):
    placed = (
        P(None, "day", "tile", None, None),
        P("day", "tile", None, None),
        P("day", "tile"),
        P(),
        P(),
        P(),
        P(),
        P(),
        P(),
        P(),
        P(),
    )
    return jax.shard_map(
        local, mesh=mesh, in_specs=placed, out_specs=P(None, "day", "tile"), check_vma=False
    )
```

```python
import functools

import jax
import jax.numpy as jnp
from jax import lax
from jax.experimental import pallas as pl
from jax.experimental.pallas import tpu as pltpu
from jax.sharding import PartitionSpec as P

BF = jnp.bfloat16
F32 = jnp.float32
HALO = 4
LANES = 128
VMEM = pl.BlockSpec(memory_space=pltpu.VMEM)
SMEM = pl.BlockSpec(memory_space=pltpu.SMEM)
HBM = pl.BlockSpec(memory_space=pltpu.HBM)


def iota(shape, dim):
    return lax.broadcasted_iota(jnp.int32, shape, dim)


def pack_kernel(tiles, bands, days, scene_ref, list_ref, out_ref, scene, wide, mixed, blocks, picked, tail, sem):
    variables, slots = scene_ref.shape[0], scene_ref.shape[1]
    copies = [pltpu.make_async_copy(scene_ref.at[v], scene.at[v], sem.at[v]) for v in range(variables)]
    for copy in copies:
        copy.start()

    def clear(i, c):
        out_ref[i] = jnp.zeros(out_ref.shape[1:], BF)
        return c

    lax.fori_loop(0, out_ref.shape[0], clear, 0)

    def clear_tail(i, c):
        tail[i] = jnp.zeros((8, LANES), F32)
        return c

    lax.fori_loop(0, tail.shape[0], clear_tail, 0)
    for v in range(variables):
        wide[v, 0:16] = jnp.zeros((16, LANES), F32)
        copies[v].wait()
        wide[v, 16 : 16 + slots] = scene[v].astype(F32)
        wide[v, 16 + slots : 32 + slots] = jnp.zeros((16, LANES), F32)
    row = iota((16, LANES), 0)

    def place(day, first):
        for band in range(bands):
            tile, offset, count = (list_ref[k, band, day] for k in range(3))
            live = (row >= offset) & (row < offset + count)
            for v in range(variables):
                rows = wide[v, pl.ds(16 + first - offset, 16), :]
                mixed[band, pl.ds(v, 16, stride=4), :] = jnp.where(live, rows, 0.0)
            block = mixed[band].astype(BF)
            blocks[day * bands + band] = block
            out_ref[band * tiles + tile, 16:80] = block
            if band + 1 < bands:
                out_ref[(band + 1) * tiles + tile, 0:16] = block[48:64]
            if band > 0:
                out_ref[(band - 1) * tiles + tile, 80:96] = block[0:16]
            first = first + count
        return first

    lax.fori_loop(0, days, place, jnp.int32(0))

    q, lane = iota((LANES, LANES), 0), iota((LANES, LANES), 1)
    edge = lane % 8
    choose = (q == jnp.where(edge < 4, 124 + edge, edge - 4)).astype(F32).astype(BF)
    granules = days * bands
    spread = jnp.dot(
        blocks[...].reshape(granules * 64, LANES), choose, preferred_element_type=F32
    ).reshape(granules, 64, LANES)
    r64, l64 = iota((64, LANES), 0), iota((64, LANES), 1)
    own = (r64 % 4 == l64 // 32) & ((r64 // 4) % 4 == (l64 % 32) // 8)
    for g in range(granules):
        kept = jnp.where(own, spread[g], 0.0)
        part = [jnp.sum(kept[16 * j : 16 * j + 16], axis=0, keepdims=True) for j in range(4)]
        zero = jnp.zeros((2, LANES), F32)
        picked[g] = jnp.concatenate([part[3], part[0], part[1], part[2], part[3], part[0], zero], 0)

    sub, col = iota((8, LANES), 0), iota((8, LANES), 1)
    row_of = {0: (sub >= 1) & (sub <= 4), 1: sub == 0, -1: sub == 5}
    is_left = col % 8 < 4
    day_base = lax.axis_index("day") * days

    def tags(day, c):
        for band in range(bands):
            tile, offset, count = (list_ref[k, band, day] for k in range(3))
            sides = picked[day * bands + band]
            for step, shift, low, high, region in ((0, 4, 0, 16, 1), (1, -12, 12, 16, 0), (-1, 20, 0, 4, 2)):
                lo, hi = jnp.maximum(offset, low), jnp.minimum(offset + count, high)
                for side in range(3):
                    r = col - (24 * side + shift)
                    tag = jnp.where(col == 72 + 3 * side + region, (day_base + day + 1).astype(F32), 0.0)
                    note = jnp.where(sub == 6, jnp.where((r >= lo) & (r < hi), 1.0, tag), 0.0)
                    if side > 0:
                        wanted = row_of[step] & (is_left if side == 1 else jnp.logical_not(is_left))
                        note = note + jnp.where(wanted, sides, 0.0)
                    at = (band + step + 1) * (tiles + 2) + tile + (1, 2, 0)[side]
                    tail[at] = tail[at] + note
        return c

    lax.fori_loop(0, days, tags, 0)
    for band in range(bands):

        def finish(tile, c, band=band):
            out_ref[band * tiles + tile, 96:104] = tail[(band + 1) * (tiles + 2) + tile + 1].astype(BF)
            return c

        lax.fori_loop(0, tiles, finish, 0)


def halves(value):
    high = value.astype(BF)
    return high, (value - high.astype(F32)).astype(BF)


def place_of(block, width, shape):
    first = block * LANES // width
    lane = iota(shape, len(shape) - 1)
    row = first + (lane >= (first + 1) * width - block * LANES).astype(jnp.int32)
    return row, lane + block * LANES - row * width


def weights_kernel(
    width,
    *refs,
):
    params, results, held, made, sem = refs[:7], refs[7:15], refs[15:22], refs[22:30], refs[30]
    copies = [pltpu.make_async_copy(a, b, sem.at[i]) for i, (a, b) in enumerate(zip(params, held))]
    for copy in copies:
        copy.start()
    for copy in copies:
        copy.wait()
    weights_body(width, *held, *made)
    copies = [pltpu.make_async_copy(a, b, sem.at[i]) for i, (a, b) in enumerate(zip(made, results))]
    for copy in copies:
        copy.start()
    for copy in copies:
        copy.wait()


def weights_body(
    width,
    taps_ref,
    time_ref,
    mix_ref,
    mix_bias_ref,
    in_ref,
    obs_bias_ref,
    out_ref,
    band_out,
    first_out,
    rest_out,
    bias_out,
    in_out,
    out_out,
    expand_out,
    valid_out,
):
    layers, channels = mix_ref.shape[0], mix_ref.shape[1]
    half = first_out.shape[0] // (2 * channels)
    days = 2 * half
    size = channels * days

    delta = [(k // 3 - 1) * width + k % 3 - 1 for k in range(9)]
    offset = iota((16, LANES), 0) - iota((16, LANES), 1)

    def band(at, c):
        l, ch = at // channels, at % channels
        taps = [taps_ref[k, l, ch] for k in range(9)]
        for t in range(5):
            for k0 in range(0, LANES, 16):
                value = jnp.zeros((16, LANES), F32)
                for tap, d in zip(taps, delta):
                    want = d - LANES * (t - 2) - k0
                    if -(LANES - 1) <= want <= 15:
                        value = jnp.where(offset == want, tap, value)
                band_out[l, ch, t, k0 : k0 + 16] = value.astype(BF)
        return c

    lax.fori_loop(0, layers * channels, band, 0)

    hot = ((iota((size, channels), 0) // half) % channels == iota((size, channels), 1)).astype(F32).astype(BF)
    day = lambda n, shape, dim: 2 * (iota(shape, dim) % half) + iota(shape, dim) // (channels * half)

    def widened(l, k, count):
        mixed = (0.5 * mix_ref[l].astype(F32) * time_ref[k, l : l + 1]).astype(BF)
        rows = jnp.dot(hot[:count], mixed, preferred_element_type=F32).astype(BF)
        return lax.dot_general(rows, hot[:count], (((1,), (1,)), ((), ())), preferred_element_type=F32)

    for l in range(layers):
        count = size if l == 0 else size // 2
        gap = day(l, (count, count), 1) - day(l, (count, count), 0)
        value = jnp.zeros((count, count), F32)
        for k in range(3):
            value = jnp.where(gap == (k - 1) * 2**l, widened(l, k, count), value)
        if l == 0:
            first_out[...] = value.astype(BF)
        else:
            rest_out[l - 1] = value.astype(BF)

    rows8 = jnp.concatenate([0.5 * mix_bias_ref[...], obs_bias_ref[...], jnp.zeros((3, channels), F32)], 0)
    high, rest = halves(rows8)
    mid, low = halves(rows8 - high.astype(F32))
    nt = lambda a, b: lax.dot_general(a, b, (((1,), (1,)), ((), ())), preferred_element_type=F32)
    column = nt(hot, high) + (nt(hot, mid) + nt(hot, low))
    for l in range(layers):
        bias_out[l] = jnp.broadcast_to(column[:, l : l + 1], (size, LANES))

    variables = in_ref.shape[0]
    repeat = (iota((variables, LANES), 1) // days == iota((variables, LANES), 0)).astype(F32).astype(BF)
    in_row = lax.dot_general(
        in_ref[...].astype(F32), repeat.astype(F32), (((0,), (0,)), ((), ())), preferred_element_type=F32
    ).astype(BF)
    wide = jnp.dot(hot, in_row, preferred_element_type=F32)
    same = day(0, (size, LANES), 0) == iota((size, LANES), 1) % days
    in_out[:, :LANES] = jnp.where(same, wide, 0.0).astype(BF)
    same = day(0, (size, days), 0) == iota((size, days), 1)
    b_high, b_low = halves(column[:, layers : layers + 1])
    for at, part in ((LANES, b_high), (LANES + days, b_low)):
        in_out[:, at : at + days] = jnp.where(
            same, jnp.broadcast_to(part.astype(F32), (size, days)), 0.0
        ).astype(BF)
    out_row = nt(jnp.broadcast_to(out_ref[...], (8, channels)), hot)
    same = iota((days, size), 0) == day(0, (days, size), 1)
    out_out[...] = jnp.where(same, jnp.broadcast_to(out_row[0:1], (days, size)), 0.0).astype(BF)

    bands, tiles = lax.axis_size("day"), lax.axis_size("tile")
    band_at, tile_at = lax.axis_index("day"), lax.axis_index("tile")
    cols, rows = width - 2 * HALO, 16
    for b in range(expand_out.shape[0]):
        row, q = place_of(b, width, (LANES, LANES))
        side = jnp.where(q < HALO, 1, jnp.where(q >= cols + HALO, 2, 0))
        hit = (24 * side + row == iota((LANES, LANES), 0)) & (row < rows + 2 * HALO)
        expand_out[b] = jnp.where(hit, 1.0, 0.0).astype(BF)
        row, q = place_of(b, width, (1, LANES))
        low_r = jnp.where(band_at == 0, HALO, 0)
        high_r = jnp.where(band_at == bands - 1, rows + HALO, rows + 2 * HALO)
        low_q = jnp.where(tile_at == 0, HALO, 0)
        high_q = jnp.where(tile_at == tiles - 1, cols + HALO, cols + 2 * HALO)
        inside = (row >= low_r) & (row < high_r) & (q >= low_q) & (q < high_q)
        valid_out[b : b + 1] = jnp.where(inside, 1.0, 0.0)


def chunked(low, high, step, fn):
    count = (high - low) // step
    spare = (high - low) - count * step
    for i in range(low, low + spare):
        fn(i)

    def body(i, c):
        for u in range(step):
            fn(low + spare + i * step + u)
        return c

    lax.fori_loop(0, count, body, 0)


def main_kernel(
    sources,
    arrived_ref,
    land_ref,
    land_left_ref,
    land_right_ref,
    own_land_ref,
    out_b_ref,
    *refs,
):
    given, out_ref, x_ref, v_ref, y_ref = refs[:8], refs[8], refs[9], refs[10], refs[11]
    held, taps_sem, sem = refs[12:20], refs[20], refs[21]
    banded_ref, first_ref, rest_ref, bias_ref, in_ref, out_w_ref, expand_ref, valid_ref = held
    copies = [pltpu.make_async_copy(given[i], held[i], sem.at[i]) for i in range(1, 8)]
    for copy in copies[::-1]:
        copy.start()
    fetch = [
        pltpu.make_async_copy(given[0].at[l], banded_ref.at[l], taps_sem.at[l]) for l in range(banded_ref.shape[0])
    ]
    for copy in fetch:
        copy.start()
    channels = banded_ref.shape[1]
    layers = banded_ref.shape[0]
    width = LANES + 2 * HALO
    rows_in = 24

    tail = arrived_ref[:, 96:104, :].astype(F32).reshape(8 * sources, LANES).astype(BF)
    pick_r, pick_c = iota((7 * sources, 8 * sources), 0), iota((7 * sources, 8 * sources), 1)
    pick = ((pick_c // 8 == pick_r % sources) & (pick_c % 8 == pick_r // sources)).astype(F32).astype(BF)
    parts = jnp.dot(pick, tail, preferred_element_type=F32).astype(BF)
    side_rows = [parts[j * sources : (j + 1) * sources] for j in range(6)]
    meta = parts[6 * sources :]
    wanted = (iota((16, LANES), 1) == iota((16, LANES), 0) + 72).astype(F32).astype(BF)
    tag_rows = lax.dot_general(wanted, meta, (((1,), (1,)), ((), ())), preferred_element_type=F32)
    repeat = (iota((sources, 8 * sources), 1) // 8 == iota((sources, 8 * sources), 0)).astype(F32).astype(BF)
    tag_wide = jnp.dot(tag_rows.astype(BF), repeat, preferred_element_type=F32)
    m, k = iota((256, 8 * sources), 0), iota((256, 8 * sources), 1)
    same = m // 32 == k % 8
    day_of = (m % 32 + 1).astype(F32)
    perms = [
        jnp.where(same & (tag_wide[b : b + 1] == day_of), 1.0, 0.0).astype(BF) for b in range(3)
    ]
    day_col = (iota((32, sources), 0) + 1).astype(F32)
    hot = [jnp.where(tag_rows[i : i + 1] == day_col, 1.0, 0.0).astype(BF) for i in range(9)]

    lane32 = iota((32, LANES), 1)
    cover = jnp.zeros((32, LANES), F32)
    for side in range(3):
        for band, (lo, hi) in enumerate(((0, 4), (4, 20), (20, 24))):
            got = jnp.dot(hot[3 * side + band], meta, preferred_element_type=F32)
            here = (lane32 >= 24 * side + lo) & (lane32 < 24 * side + hi)
            cover = jnp.where(here, got, cover)
    cover = cover.astype(BF)

    packed = [[None] * 2 for _ in range(4)]
    for j in range(6):
        band = 0 if j == 0 else (2 if j == 5 else 1)
        left = jnp.dot(hot[3 + band], side_rows[j], preferred_element_type=F32)
        right = jnp.dot(hot[6 + band], side_rows[j], preferred_element_type=F32)
        both = jnp.where(lane32 % 8 < 4, left, right)
        half, start = (32 * j) // LANES, (32 * j) % LANES
        here = (lane32 >= start) & (lane32 < start + 32)
        for v in range(4):
            moved = pltpu.roll(both, (start - 32 * v) % LANES, 1)
            had = packed[v][half]
            packed[v][half] = jnp.where(here, moved, 0.0 if had is None else had)
    edges = [jnp.concatenate([packed[v][h] for v in range(4)], 0) for h in range(2)]

    rolled = []
    for p in range(12):
        band = 0 if p < 2 else (2 if p >= 10 else 1)
        rows = arrived_ref[:, 8 * p : 8 * p + 8, :].astype(F32).reshape(8 * sources, LANES).astype(BF)
        got = jnp.dot(perms[band], rows, preferred_element_type=F32)
        for r2 in range(2):
            row = 2 * p + r2
            rolled.append(pltpu.roll(got[128 * r2 : 128 * r2 + 128], (8 * row + 4) % LANES, 1))
    lane = iota((LANES, LANES), 1)
    zero = jnp.zeros((LANES, LANES), F32)

    def flat_block(b):
        now, start = (b, 8 * b + 4) if b <= 15 else ((b - 1, 8 * b - 132) if b >= 17 else (16, 132))
        before = now - 1
        now_v = rolled[now] if now < rows_in else zero
        before_v = rolled[before] if before >= 0 else zero
        edge = edges[0] if b <= 16 else edges[1]
        return jnp.where(lane < start - 8, before_v, jnp.where(lane < start, edge, now_v))

    land, land_left, land_right = (
        pltpu.roll(
            jnp.concatenate([ref[...].astype(F32), jnp.zeros((LANES - rows_in, LANES), F32)], 0), 4, 1, stride=8, stride_axis=0
        )
        for ref in (land_ref, land_left_ref, land_right_ref)
    )
    lane1 = iota((1, LANES), 1)

    def land_block(b):
        now, start = (b, 8 * b + 4) if b <= 15 else ((b - 1, 8 * b - 132) if b >= 17 else (16, 132))
        pick = lambda a, r: a[r : r + 1] if 0 <= r < rows_in else jnp.zeros((1, LANES), F32)
        value = jnp.where(lane1 < start - 4, pick(land_right, now - 1), pick(land_left, now))
        value = jnp.where(lane1 < start - 8, pick(land, now - 1), value)
        return jnp.where(lane1 < start, value, pick(land, now))

    for copy in copies:
        copy.wait()
    for j in range(13):
        pair = []
        for b in (2 * j, 2 * j + 1):
            keep = jnp.dot(cover, expand_ref[b], preferred_element_type=F32)
            pair.append((jnp.concatenate([flat_block(b), keep, keep], 0) * land_block(b)).astype(BF))
        got = jnp.dot(in_ref[...], jnp.concatenate(pair, 1), preferred_element_type=F32).astype(BF)
        x_ref[2 * j] = got[:, :LANES]
        x_ref[2 * j + 1] = got[:, LANES:]

    for b in (0, 1, 28, 29):
        v_ref[b] = jnp.zeros(v_ref.shape[1:], BF)

    def mix(l, j):
        both = jnp.concatenate([x_ref[2 * j], x_ref[2 * j + 1]], 1)
        ok = jnp.concatenate([valid_ref[pl.ds(2 * j, 1)], valid_ref[pl.ds(2 * j + 1, 1)]], 1)
        bias = bias_ref[l]
        for p in range(2):
            half = slice(256 * p, 256 * p + 256)
            if l == 0:
                acc = jnp.dot(first_ref[half], both, preferred_element_type=F32)
            else:
                acc = jnp.dot(rest_ref[l - 1], both[half], preferred_element_type=F32)
            h = acc + jnp.concatenate([bias[half], bias[half]], 1)
            v = ((h + h * jnp.tanh(h)) * ok).astype(BF)
            v_ref[2 * j + 2, half] = v[:, :LANES]
            v_ref[2 * j + 3, half] = v[:, LANES:]

    def stencil(l, low, high, c):
        groups = [pl.ds(pl.multiple_of(c * 16 + 256 * p, 16), 16) for p in range(2)]
        lhs = jnp.concatenate(
            [
                jnp.concatenate([v_ref[2 * j + b, rows] for b in range(6)], 1)
                for j in range(low, high)
                for rows in groups
            ],
            0,
        )
        t = [jnp.zeros((LANES, LANES), BF)] + [banded_ref[l, c, i] for i in range(5)]
        t = t + [t[0]]
        rhs = jnp.concatenate([jnp.concatenate([t[a + 1], t[a]], 1) for a in range(6)], 0)
        acc = jnp.dot(lhs, rhs, preferred_element_type=F32)
        at = 0
        for j in range(low, high):
            for rows in groups:
                for h in range(2):
                    part = acc[at : at + 16, LANES * h : LANES * h + LANES]
                    x_ref[2 * j + h, rows] = (x_ref[2 * j + h, rows].astype(F32) + part).astype(BF)
                at += 16

    for l in range(layers):
        low_v, high_v = l * width // 256, -(-(rows_in - l) * width // 256)
        low_x, high_x = (l + 1) * width // 256, -(-(rows_in - l - 1) * width // 256)
        chunked(low_v, high_v, 4, functools.partial(mix, l))
        fetch[l].wait()
        chunked(0, channels, 4, functools.partial(stencil, l, low_x, high_x))

    for j in range(2, 11):
        got = jnp.dot(
            out_w_ref[...], jnp.concatenate([x_ref[2 * j], x_ref[2 * j + 1]], 1), preferred_element_type=F32
        )
        y_ref[2 * j] = got[:, :LANES]
        y_ref[2 * j + 1] = got[:, LANES:]
    lane_d = iota((32, LANES), 1)
    for r in range(16):
        block, start = divmod((r + HALO) * width + HALO, LANES)
        back = (LANES - start) % LANES
        value = pltpu.roll(y_ref[block], back, 1) if back else y_ref[block]
        if start:
            value = jnp.where(lane_d < LANES - start, value, pltpu.roll(y_ref[block + 1], back, 1))
        out_ref[:, r, :] = (value + out_b_ref[0]) * own_land_ref[r : r + 1].astype(F32)


def local(
    scene_rows,
    granule_list,
    land_mask,
    in_weight,
    obs_bias,
    time_taps,
    mix_weight,
    mix_bias,
    space_taps,
    out_weight,
    out_bias,
):
    bands = lax.axis_size("day")
    tiles = lax.axis_size("tile")
    days_here = granule_list.shape[0]
    days = days_here * bands
    rows, cols = land_mask.shape
    channels, variables = in_weight.shape
    layers = mix_weight.shape[0]
    sources = bands * tiles
    width = cols + 2 * HALO
    slots = scene_rows.shape[3]
    n_block = 26

    notes = jnp.transpose(granule_list.reshape(days_here, bands, 3), (2, 1, 0))
    granules = days_here * bands
    outgoing = pl.pallas_call(
        functools.partial(pack_kernel, tiles, bands, days_here),
        out_shape=jax.ShapeDtypeStruct((sources, 104, cols), BF),
        in_specs=[HBM, SMEM],
        out_specs=VMEM,
        scratch_shapes=[
            pltpu.VMEM((variables, slots, cols), BF),
            pltpu.VMEM((variables, slots + 32, cols), F32),
            pltpu.VMEM((bands, 64, cols), F32),
            pltpu.VMEM((granules, 64, cols), BF),
            pltpu.VMEM((granules, 8, cols), F32),
            pltpu.VMEM(((bands + 2) * (tiles + 2), 8, cols), F32),
            pltpu.SemaphoreType.DMA((variables,)),
        ],
        compiler_params=pltpu.CompilerParams(vmem_limit_bytes=60 * 2**20),
        name="pack",
    )(scene_rows.reshape(variables, slots, cols), notes)

    size = channels * days
    shape = lambda *dims, dtype=BF: jax.ShapeDtypeStruct(dims, dtype)
    land_mask, time_taps, outgoing = lax.optimization_barrier((land_mask, time_taps, outgoing))
    params = (
        jnp.transpose(space_taps, (2, 0, 1)),
        jnp.transpose(time_taps, (2, 0, 1)),
        mix_weight,
        mix_bias,
        in_weight.T,
        obs_bias.reshape(1, channels),
        out_weight.reshape(1, channels),
    )
    made = (
        shape(layers, channels, 5, LANES, LANES),
        shape(size, size),
        shape(layers - 1, size // 2, size // 2),
        shape(layers, size, LANES, dtype=F32),
        shape(size, (variables + 2) * days),
        shape(days, size),
        shape(n_block, LANES, LANES),
        shape(n_block, LANES, dtype=F32),
    )
    weights = pl.pallas_call(
        functools.partial(weights_kernel, width),
        out_shape=made,
        in_specs=[HBM] * 7,
        out_specs=(HBM,) * 8,
        scratch_shapes=[pltpu.SMEM(params[0].shape, F32)]
        + [pltpu.VMEM(a.shape, a.dtype) for a in params[1:]]
        + [pltpu.VMEM(a.shape, a.dtype) for a in made]
        + [pltpu.SemaphoreType.DMA((8,))],
        compiler_params=pltpu.CompilerParams(vmem_limit_bytes=60 * 2**20),
        cost_estimate=pl.CostEstimate(flops=2 * 10**9, bytes_accessed=24 * 2**20, transcendentals=0),
        name="weights",
    )(*params)
    arrived = lax.all_to_all(outgoing, ("day", "tile"), split_axis=0, concat_axis=0, tiled=True)

    forward = lambda n: [(i, i + 1) for i in range(n - 1)]
    backward = lambda n: [(i + 1, i) for i in range(n - 1)]
    land = land_mask.astype(BF)
    land = jnp.concatenate(
        [
            lax.ppermute(land[rows - HALO :], "day", forward(bands)),
            land,
            lax.ppermute(land[:HALO], "day", backward(bands)),
        ],
        0,
    )
    land_left = lax.ppermute(land, "tile", forward(tiles))
    land_right = lax.ppermute(land, "tile", backward(tiles))

    return pl.pallas_call(
        functools.partial(main_kernel, sources),
        out_shape=jax.ShapeDtypeStruct((days, rows, cols), F32),
        in_specs=[VMEM] * 5 + [SMEM] + [HBM] * 8,
        out_specs=VMEM,
        scratch_shapes=[
            pltpu.VMEM((n_block, channels * days, LANES), BF),
            pltpu.VMEM((n_block + 4, channels * days, LANES), BF),
            pltpu.VMEM((n_block, days, LANES), F32),
        ]
        + [pltpu.VMEM(a.shape, a.dtype) for a in made]
        + [pltpu.SemaphoreType.DMA((layers,)), pltpu.SemaphoreType.DMA((8,))],
        compiler_params=pltpu.CompilerParams(vmem_limit_bytes=60 * 2**20),
        name="blocks",
    )(
        arrived,
        land,
        land_left,
        land_right,
        land_mask,
        out_bias,
        *weights,
    )


def solution(mesh):
    placed = (
        P(None, "day", "tile", None, None),
        P("day", "tile", None, None),
        P("day", "tile"),
        P(),
        P(),
        P(),
        P(),
        P(),
        P(),
        P(),
        P(),
    )
    return jax.shard_map(
        local, mesh=mesh, in_specs=placed, out_specs=P(None, "day", "tile"), check_vma=False
    )
```

```python
import functools

import jax
import jax.numpy as jnp
from jax import lax
from jax.experimental import pallas as pl
from jax.experimental.pallas import tpu as pltpu
from jax.sharding import PartitionSpec as P

BF = jnp.bfloat16
F32 = jnp.float32
HALO = 4
LANES = 128
VMEM = pl.BlockSpec(memory_space=pltpu.VMEM)
SMEM = pl.BlockSpec(memory_space=pltpu.SMEM)
HBM = pl.BlockSpec(memory_space=pltpu.HBM)


def iota(shape, dim):
    return lax.broadcasted_iota(jnp.int32, shape, dim)


def pack_kernel(tiles, bands, days, scene_ref, list_ref, out_ref, scene, wide, mixed, blocks, picked, tail, sem):
    variables, slots = scene_ref.shape[0], scene_ref.shape[1]
    copies = [pltpu.make_async_copy(scene_ref.at[v], scene.at[v], sem.at[v]) for v in range(variables)]
    for copy in copies:
        copy.start()

    def clear(i, c):
        out_ref[i] = jnp.zeros(out_ref.shape[1:], BF)
        return c

    lax.fori_loop(0, out_ref.shape[0], clear, 0)

    def clear_tail(i, c):
        tail[i] = jnp.zeros((8, LANES), F32)
        return c

    lax.fori_loop(0, tail.shape[0], clear_tail, 0)
    for v in range(variables):
        wide[v, 0:16] = jnp.zeros((16, LANES), F32)
        copies[v].wait()
        wide[v, 16 : 16 + slots] = scene[v].astype(F32)
        wide[v, 16 + slots : 32 + slots] = jnp.zeros((16, LANES), F32)
    row = iota((16, LANES), 0)

    def place(day, first):
        for band in range(bands):
            tile, offset, count = (list_ref[k, band, day] for k in range(3))
            live = (row >= offset) & (row < offset + count)
            for v in range(variables):
                rows = wide[v, pl.ds(16 + first - offset, 16), :]
                mixed[band, pl.ds(v, 16, stride=4), :] = jnp.where(live, rows, 0.0)
            block = mixed[band].astype(BF)
            blocks[day * bands + band] = block
            out_ref[band * tiles + tile, 16:80] = block
            if band + 1 < bands:
                out_ref[(band + 1) * tiles + tile, 0:16] = block[48:64]
            if band > 0:
                out_ref[(band - 1) * tiles + tile, 80:96] = block[0:16]
            first = first + count
        return first

    lax.fori_loop(0, days, place, jnp.int32(0))

    q, lane = iota((LANES, LANES), 0), iota((LANES, LANES), 1)
    edge = lane % 8
    choose = (q == jnp.where(edge < 4, 124 + edge, edge - 4)).astype(F32).astype(BF)
    granules = days * bands
    spread = jnp.dot(
        blocks[...].reshape(granules * 64, LANES), choose, preferred_element_type=F32
    ).reshape(granules, 64, LANES)
    r64, l64 = iota((64, LANES), 0), iota((64, LANES), 1)
    own = (r64 % 4 == l64 // 32) & ((r64 // 4) % 4 == (l64 % 32) // 8)
    for g in range(granules):
        kept = jnp.where(own, spread[g], 0.0)
        part = [jnp.sum(kept[16 * j : 16 * j + 16], axis=0, keepdims=True) for j in range(4)]
        zero = jnp.zeros((2, LANES), F32)
        picked[g] = jnp.concatenate([part[3], part[0], part[1], part[2], part[3], part[0], zero], 0)

    sub, col = iota((8, LANES), 0), iota((8, LANES), 1)
    row_of = {0: (sub >= 1) & (sub <= 4), 1: sub == 0, -1: sub == 5}
    is_left = col % 8 < 4
    day_base = lax.axis_index("day") * days

    def tags(day, c):
        for band in range(bands):
            tile, offset, count = (list_ref[k, band, day] for k in range(3))
            sides = picked[day * bands + band]
            for step, shift, low, high, region in ((0, 4, 0, 16, 1), (1, -12, 12, 16, 0), (-1, 20, 0, 4, 2)):
                lo, hi = jnp.maximum(offset, low), jnp.minimum(offset + count, high)
                for side in range(3):
                    r = col - (24 * side + shift)
                    tag = jnp.where(col == 72 + 3 * side + region, (day_base + day + 1).astype(F32), 0.0)
                    note = jnp.where(sub == 6, jnp.where((r >= lo) & (r < hi), 1.0, tag), 0.0)
                    if side > 0:
                        wanted = row_of[step] & (is_left if side == 1 else jnp.logical_not(is_left))
                        note = note + jnp.where(wanted, sides, 0.0)
                    at = (band + step + 1) * (tiles + 2) + tile + (1, 2, 0)[side]
                    tail[at] = tail[at] + note
        return c

    lax.fori_loop(0, days, tags, 0)
    for band in range(bands):

        def finish(tile, c, band=band):
            out_ref[band * tiles + tile, 96:104] = tail[(band + 1) * (tiles + 2) + tile + 1].astype(BF)
            return c

        lax.fori_loop(0, tiles, finish, 0)


def halves(value):
    high = value.astype(BF)
    return high, (value - high.astype(F32)).astype(BF)


def place_of(block, width, shape):
    first = block * LANES // width
    lane = iota(shape, len(shape) - 1)
    row = first + (lane >= (first + 1) * width - block * LANES).astype(jnp.int32)
    return row, lane + block * LANES - row * width


def weights_kernel(
    width,
    *refs,
):
    params, results, held, made, sem = refs[:7], refs[7:15], refs[15:22], refs[22:30], refs[30]
    copies = [pltpu.make_async_copy(a, b, sem.at[i]) for i, (a, b) in enumerate(zip(params, held))]
    for copy in copies:
        copy.start()
    for copy in copies:
        copy.wait()
    weights_body(width, *held, *made)
    copies = [pltpu.make_async_copy(a, b, sem.at[i]) for i, (a, b) in enumerate(zip(made, results))]
    for copy in copies:
        copy.start()
    for copy in copies:
        copy.wait()


def weights_body(
    width,
    taps_ref,
    time_ref,
    mix_ref,
    mix_bias_ref,
    in_ref,
    obs_bias_ref,
    out_ref,
    band_out,
    first_out,
    rest_out,
    bias_out,
    in_out,
    out_out,
    expand_out,
    valid_out,
):
    layers, channels = mix_ref.shape[0], mix_ref.shape[1]
    half = first_out.shape[0] // (2 * channels)
    days = 2 * half
    size = channels * days

    delta = [(k // 3 - 1) * width + k % 3 - 1 for k in range(9)]
    offset = iota((16, LANES), 0) - iota((16, LANES), 1)

    def band(at, c):
        l, ch = at // channels, at % channels
        taps = [taps_ref[k, l, ch] for k in range(9)]
        for t in range(5):
            for k0 in range(0, LANES, 16):
                value = jnp.zeros((16, LANES), F32)
                for tap, d in zip(taps, delta):
                    want = d - LANES * (t - 2) - k0
                    if -(LANES - 1) <= want <= 15:
                        value = jnp.where(offset == want, tap, value)
                band_out[l, ch, t, k0 : k0 + 16] = value.astype(BF)
        return c

    lax.fori_loop(0, layers * channels, band, 0)

    hot = ((iota((size, channels), 0) // half) % channels == iota((size, channels), 1)).astype(F32).astype(BF)
    day = lambda n, shape, dim: 2 * (iota(shape, dim) % half) + iota(shape, dim) // (channels * half)

    def widened(l, k, count):
        mixed = (0.5 * mix_ref[l].astype(F32) * time_ref[k, l : l + 1]).astype(BF)
        rows = jnp.dot(hot[:count], mixed, preferred_element_type=F32).astype(BF)
        return lax.dot_general(rows, hot[:count], (((1,), (1,)), ((), ())), preferred_element_type=F32)

    for l in range(layers):
        count = size if l == 0 else size // 2
        gap = day(l, (count, count), 1) - day(l, (count, count), 0)
        value = jnp.zeros((count, count), F32)
        for k in range(3):
            value = jnp.where(gap == (k - 1) * 2**l, widened(l, k, count), value)
        if l == 0:
            first_out[...] = value.astype(BF)
        else:
            rest_out[l - 1] = value.astype(BF)

    rows8 = jnp.concatenate([0.5 * mix_bias_ref[...], obs_bias_ref[...], jnp.zeros((3, channels), F32)], 0)
    high, rest = halves(rows8)
    mid, low = halves(rows8 - high.astype(F32))
    nt = lambda a, b: lax.dot_general(a, b, (((1,), (1,)), ((), ())), preferred_element_type=F32)
    column = nt(hot, high) + (nt(hot, mid) + nt(hot, low))
    for l in range(layers):
        bias_out[l] = jnp.broadcast_to(column[:, l : l + 1], (size, LANES))

    variables = in_ref.shape[0]
    repeat = (iota((variables, LANES), 1) // days == iota((variables, LANES), 0)).astype(F32).astype(BF)
    in_row = lax.dot_general(
        in_ref[...].astype(F32), repeat.astype(F32), (((0,), (0,)), ((), ())), preferred_element_type=F32
    ).astype(BF)
    wide = jnp.dot(hot, in_row, preferred_element_type=F32)
    same = day(0, (size, LANES), 0) == iota((size, LANES), 1) % days
    in_out[:, :LANES] = jnp.where(same, wide, 0.0).astype(BF)
    same = day(0, (size, days), 0) == iota((size, days), 1)
    b_high, b_low = halves(column[:, layers : layers + 1])
    for at, part in ((LANES, b_high), (LANES + days, b_low)):
        in_out[:, at : at + days] = jnp.where(
            same, jnp.broadcast_to(part.astype(F32), (size, days)), 0.0
        ).astype(BF)
    out_row = nt(jnp.broadcast_to(out_ref[...], (8, channels)), hot)
    same = iota((days, size), 0) == day(0, (days, size), 1)
    out_out[...] = jnp.where(same, jnp.broadcast_to(out_row[0:1], (days, size)), 0.0).astype(BF)

    bands, tiles = lax.axis_size("day"), lax.axis_size("tile")
    band_at, tile_at = lax.axis_index("day"), lax.axis_index("tile")
    cols, rows = width - 2 * HALO, 16
    for b in range(expand_out.shape[0]):
        row, q = place_of(b, width, (LANES, LANES))
        side = jnp.where(q < HALO, 1, jnp.where(q >= cols + HALO, 2, 0))
        hit = (24 * side + row == iota((LANES, LANES), 0)) & (row < rows + 2 * HALO)
        expand_out[b] = jnp.where(hit, 1.0, 0.0).astype(BF)
        row, q = place_of(b, width, (1, LANES))
        low_r = jnp.where(band_at == 0, HALO, 0)
        high_r = jnp.where(band_at == bands - 1, rows + HALO, rows + 2 * HALO)
        low_q = jnp.where(tile_at == 0, HALO, 0)
        high_q = jnp.where(tile_at == tiles - 1, cols + HALO, cols + 2 * HALO)
        inside = (row >= low_r) & (row < high_r) & (q >= low_q) & (q < high_q)
        valid_out[b : b + 1] = jnp.where(inside, 1.0, 0.0)


def main_kernel(
    sources,
    arrived_ref,
    land_ref,
    land_left_ref,
    land_right_ref,
    own_land_ref,
    out_b_ref,
    *refs,
):
    given, out_ref, x_ref, v_ref, y_ref = refs[:8], refs[8], refs[9], refs[10], refs[11]
    held, taps_sem, sem = refs[12:20], refs[20], refs[21]
    banded_ref, first_ref, rest_ref, bias_ref, in_ref, out_w_ref, expand_ref, valid_ref = held
    copies = [pltpu.make_async_copy(given[i], held[i], sem.at[i]) for i in range(1, 8)]
    for copy in copies[::-1]:
        copy.start()
    fetch = [
        pltpu.make_async_copy(given[0].at[l], banded_ref.at[l], taps_sem.at[l]) for l in range(banded_ref.shape[0])
    ]
    channels = banded_ref.shape[1]
    layers = banded_ref.shape[0]
    width = LANES + 2 * HALO
    rows_in = 24

    tail = arrived_ref[:, 96:104, :].astype(F32).reshape(8 * sources, LANES).astype(BF)
    pick_r, pick_c = iota((7 * sources, 8 * sources), 0), iota((7 * sources, 8 * sources), 1)
    pick = ((pick_c // 8 == pick_r % sources) & (pick_c % 8 == pick_r // sources)).astype(F32).astype(BF)
    parts = jnp.dot(pick, tail, preferred_element_type=F32).astype(BF)
    side_rows = [parts[j * sources : (j + 1) * sources] for j in range(6)]
    meta = parts[6 * sources :]
    wanted = (iota((16, LANES), 1) == iota((16, LANES), 0) + 72).astype(F32).astype(BF)
    tag_rows = lax.dot_general(wanted, meta, (((1,), (1,)), ((), ())), preferred_element_type=F32)
    repeat = (iota((sources, 8 * sources), 1) // 8 == iota((sources, 8 * sources), 0)).astype(F32).astype(BF)
    tag_wide = jnp.dot(tag_rows.astype(BF), repeat, preferred_element_type=F32)
    m, k = iota((256, 8 * sources), 0), iota((256, 8 * sources), 1)
    same = m // 32 == k % 8
    day_of = (m % 32 + 1).astype(F32)
    perms = [
        jnp.where(same & (tag_wide[b : b + 1] == day_of), 1.0, 0.0).astype(BF) for b in range(3)
    ]
    day_col = (iota((32, sources), 0) + 1).astype(F32)
    hot = [jnp.where(tag_rows[i : i + 1] == day_col, 1.0, 0.0).astype(BF) for i in range(9)]

    lane32 = iota((32, LANES), 1)
    cover = jnp.zeros((32, LANES), F32)
    for side in range(3):
        for band, (lo, hi) in enumerate(((0, 4), (4, 20), (20, 24))):
            got = jnp.dot(hot[3 * side + band], meta, preferred_element_type=F32)
            here = (lane32 >= 24 * side + lo) & (lane32 < 24 * side + hi)
            cover = jnp.where(here, got, cover)
    cover = cover.astype(BF)

    packed = [[None] * 2 for _ in range(4)]
    for j in range(6):
        band = 0 if j == 0 else (2 if j == 5 else 1)
        left = jnp.dot(hot[3 + band], side_rows[j], preferred_element_type=F32)
        right = jnp.dot(hot[6 + band], side_rows[j], preferred_element_type=F32)
        both = jnp.where(lane32 % 8 < 4, left, right)
        half, start = (32 * j) // LANES, (32 * j) % LANES
        here = (lane32 >= start) & (lane32 < start + 32)
        for v in range(4):
            moved = pltpu.roll(both, (start - 32 * v) % LANES, 1)
            had = packed[v][half]
            packed[v][half] = jnp.where(here, moved, 0.0 if had is None else had)
    edges = [jnp.concatenate([packed[v][h] for v in range(4)], 0) for h in range(2)]

    rolled = []
    pairs = []
    for p in range(0, 12, 2):
        band = 0 if p < 2 else (2 if p >= 10 else 1)
        rows = [
            arrived_ref[:, 8 * i : 8 * i + 8, :].astype(F32).reshape(8 * sources, LANES).astype(BF)
            for i in (p, p + 1)
        ]
        both = jnp.dot(perms[band], jnp.concatenate(rows, 1), preferred_element_type=F32)
        pairs += [both[:, :LANES], both[:, LANES:]]
    for p, got in enumerate(pairs):
        for r2 in range(2):
            row = 2 * p + r2
            rolled.append(pltpu.roll(got[128 * r2 : 128 * r2 + 128], (8 * row + 4) % LANES, 1))
    lane = iota((LANES, LANES), 1)
    zero = jnp.zeros((LANES, LANES), F32)

    def flat_block(b):
        now, start = (b, 8 * b + 4) if b <= 15 else ((b - 1, 8 * b - 132) if b >= 17 else (16, 132))
        before = now - 1
        now_v = rolled[now] if now < rows_in else zero
        before_v = rolled[before] if before >= 0 else zero
        edge = edges[0] if b <= 16 else edges[1]
        return jnp.where(lane < start - 8, before_v, jnp.where(lane < start, edge, now_v))

    land, land_left, land_right = (
        pltpu.roll(
            jnp.concatenate([ref[...].astype(F32), jnp.zeros((LANES - rows_in, LANES), F32)], 0), 4, 1, stride=8, stride_axis=0
        )
        for ref in (land_ref, land_left_ref, land_right_ref)
    )
    lane1 = iota((1, LANES), 1)

    def land_block(b):
        now, start = (b, 8 * b + 4) if b <= 15 else ((b - 1, 8 * b - 132) if b >= 17 else (16, 132))
        pick = lambda a, r: a[r : r + 1] if 0 <= r < rows_in else jnp.zeros((1, LANES), F32)
        value = jnp.where(lane1 < start - 4, pick(land_right, now - 1), pick(land_left, now))
        value = jnp.where(lane1 < start - 8, pick(land, now - 1), value)
        return jnp.where(lane1 < start, value, pick(land, now))

    for copy in copies:
        copy.wait()
    for copy in fetch:
        copy.start()
    for j in range(13):
        pair = []
        for b in (2 * j, 2 * j + 1):
            keep = jnp.dot(cover, expand_ref[b], preferred_element_type=F32)
            pair.append((jnp.concatenate([flat_block(b), keep, keep], 0) * land_block(b)).astype(BF))
        got = jnp.dot(in_ref[...], jnp.concatenate(pair, 1), preferred_element_type=F32).astype(BF)
        x_ref[2 * j] = got[:, :LANES]
        x_ref[2 * j + 1] = got[:, LANES:]

    for b in (0, 1, 28, 29):
        v_ref[b] = jnp.zeros(v_ref.shape[1:], BF)

    def mix(l, j):
        both = jnp.concatenate([x_ref[2 * j], x_ref[2 * j + 1]], 1)
        ok = jnp.concatenate([valid_ref[2 * j : 2 * j + 1], valid_ref[2 * j + 1 : 2 * j + 2]], 1)
        bias = bias_ref[l]
        for p in range(2):
            half = slice(256 * p, 256 * p + 256)
            if l == 0:
                acc = jnp.dot(first_ref[half], both, preferred_element_type=F32)
            else:
                acc = jnp.dot(rest_ref[l - 1], both[half], preferred_element_type=F32)
            h = acc + jnp.concatenate([bias[half], bias[half]], 1)
            v = ((h + h * jnp.tanh(h)) * ok).astype(BF)
            v_ref[2 * j + 2, half] = v[:, :LANES]
            v_ref[2 * j + 3, half] = v[:, LANES:]

    def stencil(l, low, high, c):
        groups = [slice(c * 16 + 256 * p, c * 16 + 256 * p + 16) for p in range(2)]
        lhs = jnp.concatenate(
            [
                jnp.concatenate([v_ref[2 * j + b, rows] for b in range(6)], 1)
                for j in range(low, high)
                for rows in groups
            ],
            0,
        )
        t = [jnp.zeros((LANES, LANES), BF)] + [banded_ref[l, c, i] for i in range(5)]
        t = t + [t[0]]
        rhs = jnp.concatenate([jnp.concatenate([t[a + 1], t[a]], 1) for a in range(6)], 0)
        acc = jnp.dot(lhs, rhs, preferred_element_type=F32)
        at = 0
        for j in range(low, high):
            for rows in groups:
                for h in range(2):
                    part = acc[at : at + 16, LANES * h : LANES * h + LANES]
                    x_ref[2 * j + h, rows] = (x_ref[2 * j + h, rows].astype(F32) + part).astype(BF)
                at += 16

    for l in range(layers):
        low_v, high_v = l * width // 256, -(-(rows_in - l) * width // 256)
        low_x, high_x = (l + 1) * width // 256, -(-(rows_in - l - 1) * width // 256)
        for j in range(low_v, high_v):
            mix(l, j)
        fetch[l].wait()
        for c in range(channels):
            stencil(l, low_x, high_x, c)

    for j in range(2, 11):
        got = jnp.dot(
            out_w_ref[...], jnp.concatenate([x_ref[2 * j], x_ref[2 * j + 1]], 1), preferred_element_type=F32
        )
        y_ref[2 * j] = got[:, :LANES]
        y_ref[2 * j + 1] = got[:, LANES:]
    lane_d = iota((32, LANES), 1)
    for r in range(16):
        block, start = divmod((r + HALO) * width + HALO, LANES)
        back = (LANES - start) % LANES
        value = pltpu.roll(y_ref[block], back, 1) if back else y_ref[block]
        if start:
            value = jnp.where(lane_d < LANES - start, value, pltpu.roll(y_ref[block + 1], back, 1))
        out_ref[:, r, :] = (value + out_b_ref[0]) * own_land_ref[r : r + 1].astype(F32)


def local(
    scene_rows,
    granule_list,
    land_mask,
    in_weight,
    obs_bias,
    time_taps,
    mix_weight,
    mix_bias,
    space_taps,
    out_weight,
    out_bias,
):
    bands = lax.axis_size("day")
    tiles = lax.axis_size("tile")
    days_here = granule_list.shape[0]
    days = days_here * bands
    rows, cols = land_mask.shape
    channels, variables = in_weight.shape
    layers = mix_weight.shape[0]
    sources = bands * tiles
    width = cols + 2 * HALO
    slots = scene_rows.shape[3]
    n_block = 26

    notes = jnp.transpose(granule_list.reshape(days_here, bands, 3), (2, 1, 0))
    granules = days_here * bands
    outgoing = pl.pallas_call(
        functools.partial(pack_kernel, tiles, bands, days_here),
        out_shape=jax.ShapeDtypeStruct((sources, 104, cols), BF),
        in_specs=[HBM, SMEM],
        out_specs=VMEM,
        scratch_shapes=[
            pltpu.VMEM((variables, slots, cols), BF),
            pltpu.VMEM((variables, slots + 32, cols), F32),
            pltpu.VMEM((bands, 64, cols), F32),
            pltpu.VMEM((granules, 64, cols), BF),
            pltpu.VMEM((granules, 8, cols), F32),
            pltpu.VMEM(((bands + 2) * (tiles + 2), 8, cols), F32),
            pltpu.SemaphoreType.DMA((variables,)),
        ],
        compiler_params=pltpu.CompilerParams(vmem_limit_bytes=60 * 2**20),
        name="pack",
    )(scene_rows.reshape(variables, slots, cols), notes)

    size = channels * days
    shape = lambda *dims, dtype=BF: jax.ShapeDtypeStruct(dims, dtype)
    land_mask, time_taps, outgoing = lax.optimization_barrier((land_mask, time_taps, outgoing))
    params = (
        jnp.transpose(space_taps, (2, 0, 1)),
        jnp.transpose(time_taps, (2, 0, 1)),
        mix_weight,
        mix_bias,
        in_weight.T,
        obs_bias.reshape(1, channels),
        out_weight.reshape(1, channels),
    )
    made = (
        shape(layers, channels, 5, LANES, LANES),
        shape(size, size),
        shape(layers - 1, size // 2, size // 2),
        shape(layers, size, LANES, dtype=F32),
        shape(size, (variables + 2) * days),
        shape(days, size),
        shape(n_block, LANES, LANES),
        shape(n_block, LANES, dtype=F32),
    )
    weights = pl.pallas_call(
        functools.partial(weights_kernel, width),
        out_shape=made,
        in_specs=[HBM] * 7,
        out_specs=(HBM,) * 8,
        scratch_shapes=[pltpu.SMEM(params[0].shape, F32)]
        + [pltpu.VMEM(a.shape, a.dtype) for a in params[1:]]
        + [pltpu.VMEM(a.shape, a.dtype) for a in made]
        + [pltpu.SemaphoreType.DMA((8,))],
        compiler_params=pltpu.CompilerParams(vmem_limit_bytes=60 * 2**20),
        cost_estimate=pl.CostEstimate(flops=2 * 10**9, bytes_accessed=24 * 2**20, transcendentals=0),
        name="weights",
    )(*params)
    arrived = lax.all_to_all(outgoing, ("day", "tile"), split_axis=0, concat_axis=0, tiled=True)

    forward = lambda n: [(i, i + 1) for i in range(n - 1)]
    backward = lambda n: [(i + 1, i) for i in range(n - 1)]
    land = land_mask.astype(BF)
    land = jnp.concatenate(
        [
            lax.ppermute(land[rows - HALO :], "day", forward(bands)),
            land,
            lax.ppermute(land[:HALO], "day", backward(bands)),
        ],
        0,
    )
    land_left = lax.ppermute(land, "tile", forward(tiles))
    land_right = lax.ppermute(land, "tile", backward(tiles))

    return pl.pallas_call(
        functools.partial(main_kernel, sources),
        out_shape=jax.ShapeDtypeStruct((days, rows, cols), F32),
        in_specs=[VMEM] * 5 + [SMEM] + [HBM] * 8,
        out_specs=VMEM,
        scratch_shapes=[
            pltpu.VMEM((n_block, channels * days, LANES), BF),
            pltpu.VMEM((n_block + 4, channels * days, LANES), BF),
            pltpu.VMEM((n_block, days, LANES), F32),
        ]
        + [pltpu.VMEM(a.shape, a.dtype) for a in made]
        + [pltpu.SemaphoreType.DMA((layers,)), pltpu.SemaphoreType.DMA((8,))],
        compiler_params=pltpu.CompilerParams(vmem_limit_bytes=60 * 2**20),
        name="blocks",
    )(
        arrived,
        land,
        land_left,
        land_right,
        land_mask,
        out_bias,
        *weights,
    )


def solution(mesh):
    placed = (
        P(None, "day", "tile", None, None),
        P("day", "tile", None, None),
        P("day", "tile"),
        P(),
        P(),
        P(),
        P(),
        P(),
        P(),
        P(),
        P(),
    )
    return jax.shard_map(
        local, mesh=mesh, in_specs=placed, out_specs=P(None, "day", "tile"), check_vma=False
    )
```

```python
import functools

import jax
import jax.numpy as jnp
from jax import lax
from jax.experimental import pallas as pl
from jax.experimental.pallas import tpu as pltpu
from jax.sharding import PartitionSpec as P

BF = jnp.bfloat16
F32 = jnp.float32
HALO = 4
LANES = 128
VMEM = pl.BlockSpec(memory_space=pltpu.VMEM)
SMEM = pl.BlockSpec(memory_space=pltpu.SMEM)
HBM = pl.BlockSpec(memory_space=pltpu.HBM)


def iota(shape, dim):
    return lax.broadcasted_iota(jnp.int32, shape, dim)


def pack_kernel(tiles, bands, days, scene_ref, list_ref, out_ref, scene, wide, mixed, blocks, picked, tail, sem):
    variables, slots = scene_ref.shape[0], scene_ref.shape[1]
    copies = [pltpu.make_async_copy(scene_ref.at[v], scene.at[v], sem.at[v]) for v in range(variables)]
    for copy in copies:
        copy.start()

    def clear(i, c):
        out_ref[i] = jnp.zeros(out_ref.shape[1:], BF)
        return c

    lax.fori_loop(0, out_ref.shape[0], clear, 0)

    def clear_tail(i, c):
        tail[i] = jnp.zeros((8, LANES), F32)
        return c

    lax.fori_loop(0, tail.shape[0], clear_tail, 0)
    for v in range(variables):
        wide[v, 0:16] = jnp.zeros((16, LANES), F32)
        copies[v].wait()
        wide[v, 16 : 16 + slots] = scene[v].astype(F32)
        wide[v, 16 + slots : 32 + slots] = jnp.zeros((16, LANES), F32)
    row = iota((16, LANES), 0)

    def place(day, first):
        for band in range(bands):
            tile, offset, count = (list_ref[k, band, day] for k in range(3))
            live = (row >= offset) & (row < offset + count)
            for v in range(variables):
                rows = wide[v, pl.ds(16 + first - offset, 16), :]
                mixed[band, pl.ds(v, 16, stride=4), :] = jnp.where(live, rows, 0.0)
            block = mixed[band].astype(BF)
            blocks[day * bands + band] = block
            out_ref[band * tiles + tile, 16:80] = block
            if band + 1 < bands:
                out_ref[(band + 1) * tiles + tile, 0:16] = block[48:64]
            if band > 0:
                out_ref[(band - 1) * tiles + tile, 80:96] = block[0:16]
            first = first + count
        return first

    lax.fori_loop(0, days, place, jnp.int32(0))

    q, lane = iota((LANES, LANES), 0), iota((LANES, LANES), 1)
    edge = lane % 8
    choose = (q == jnp.where(edge < 4, 124 + edge, edge - 4)).astype(F32).astype(BF)
    granules = days * bands
    spread = jnp.dot(
        blocks[...].reshape(granules * 64, LANES), choose, preferred_element_type=F32
    ).reshape(granules, 64, LANES)
    r64, l64 = iota((64, LANES), 0), iota((64, LANES), 1)
    own = (r64 % 4 == l64 // 32) & ((r64 // 4) % 4 == (l64 % 32) // 8)
    for g in range(granules):
        kept = jnp.where(own, spread[g], 0.0)
        part = [jnp.sum(kept[16 * j : 16 * j + 16], axis=0, keepdims=True) for j in range(4)]
        zero = jnp.zeros((2, LANES), F32)
        picked[g] = jnp.concatenate([part[3], part[0], part[1], part[2], part[3], part[0], zero], 0)

    sub, col = iota((8, LANES), 0), iota((8, LANES), 1)
    row_of = {0: (sub >= 1) & (sub <= 4), 1: sub == 0, -1: sub == 5}
    is_left = col % 8 < 4
    day_base = lax.axis_index("day") * days

    def tags(day, c):
        for band in range(bands):
            tile, offset, count = (list_ref[k, band, day] for k in range(3))
            sides = picked[day * bands + band]
            for step, shift, low, high, region in ((0, 4, 0, 16, 1), (1, -12, 12, 16, 0), (-1, 20, 0, 4, 2)):
                lo, hi = jnp.maximum(offset, low), jnp.minimum(offset + count, high)
                for side in range(3):
                    r = col - (24 * side + shift)
                    tag = jnp.where(col == 72 + 3 * side + region, (day_base + day + 1).astype(F32), 0.0)
                    note = jnp.where(sub == 6, jnp.where((r >= lo) & (r < hi), 1.0, tag), 0.0)
                    if side > 0:
                        wanted = row_of[step] & (is_left if side == 1 else jnp.logical_not(is_left))
                        note = note + jnp.where(wanted, sides, 0.0)
                    at = (band + step + 1) * (tiles + 2) + tile + (1, 2, 0)[side]
                    tail[at] = tail[at] + note
        return c

    lax.fori_loop(0, days, tags, 0)
    for band in range(bands):

        def finish(tile, c, band=band):
            out_ref[band * tiles + tile, 96:104] = tail[(band + 1) * (tiles + 2) + tile + 1].astype(BF)
            return c

        lax.fori_loop(0, tiles, finish, 0)


def halves(value):
    high = value.astype(BF)
    return high, (value - high.astype(F32)).astype(BF)


def place_of(block, width, shape):
    first = block * LANES // width
    lane = iota(shape, len(shape) - 1)
    row = first + (lane >= (first + 1) * width - block * LANES).astype(jnp.int32)
    return row, lane + block * LANES - row * width


def weights_kernel(
    width,
    *refs,
):
    params, results, held, made, sem = refs[:7], refs[7:14], refs[14:21], refs[21:28], refs[28]
    copies = [pltpu.make_async_copy(a, b, sem.at[i]) for i, (a, b) in enumerate(zip(params, held))]
    for copy in copies:
        copy.start()
    for copy in copies:
        copy.wait()
    weights_body(width, *held, *made)
    copies = [pltpu.make_async_copy(a, b, sem.at[i]) for i, (a, b) in enumerate(zip(made, results))]
    for copy in copies:
        copy.start()
    for copy in copies:
        copy.wait()


def weights_body(
    width,
    taps_ref,
    time_ref,
    mix_ref,
    mix_bias_ref,
    in_ref,
    obs_bias_ref,
    out_ref,
    band_out,
    first_out,
    rest_out,
    bias_out,
    in_out,
    out_out,
    valid_out,
):
    layers, channels = mix_ref.shape[0], mix_ref.shape[1]
    half = first_out.shape[0] // (2 * channels)
    days = 2 * half
    size = channels * days

    delta = [(k // 3 - 1) * width + k % 3 - 1 for k in range(9)]
    offset = iota((16, LANES), 0) - iota((16, LANES), 1)

    def band(at, c):
        l, ch = at // channels, at % channels
        taps = [taps_ref[k, l, ch] for k in range(9)]
        for t in range(5):
            for k0 in range(0, LANES, 16):
                value = jnp.zeros((16, LANES), F32)
                for tap, d in zip(taps, delta):
                    want = d - LANES * (t - 2) - k0
                    if -(LANES - 1) <= want <= 15:
                        value = jnp.where(offset == want, tap, value)
                band_out[l, ch, t, k0 : k0 + 16] = value.astype(BF)
        return c

    lax.fori_loop(0, layers * channels, band, 0)

    hot = ((iota((size, channels), 0) // half) % channels == iota((size, channels), 1)).astype(F32).astype(BF)
    day = lambda n, shape, dim: 2 * (iota(shape, dim) % half) + iota(shape, dim) // (channels * half)

    def widened(l, k, count):
        mixed = (0.5 * mix_ref[l].astype(F32) * time_ref[k, l : l + 1]).astype(BF)
        rows = jnp.dot(hot[:count], mixed, preferred_element_type=F32).astype(BF)
        return lax.dot_general(rows, hot[:count], (((1,), (1,)), ((), ())), preferred_element_type=F32)

    for l in range(layers):
        count = size if l == 0 else size // 2
        gap = day(l, (count, count), 1) - day(l, (count, count), 0)
        value = jnp.zeros((count, count), F32)
        for k in range(3):
            value = jnp.where(gap == (k - 1) * 2**l, widened(l, k, count), value)
        if l == 0:
            first_out[...] = value.astype(BF)
        else:
            rest_out[l - 1] = value.astype(BF)

    spare = jnp.zeros((LANES - layers - 1, channels), F32)
    rows8 = jnp.concatenate([0.5 * mix_bias_ref[...], obs_bias_ref[...], spare], 0)
    high, rest = halves(rows8)
    mid, low = halves(rows8 - high.astype(F32))
    nt = lambda a, b: lax.dot_general(a, b, (((1,), (1,)), ((), ())), preferred_element_type=F32)
    column = nt(hot, high) + (nt(hot, mid) + nt(hot, low))
    bias_out[...] = column

    variables = in_ref.shape[0]
    repeat = (iota((variables, LANES), 1) // days == iota((variables, LANES), 0)).astype(F32).astype(BF)
    in_row = lax.dot_general(
        in_ref[...].astype(F32), repeat.astype(F32), (((0,), (0,)), ((), ())), preferred_element_type=F32
    ).astype(BF)
    wide = jnp.dot(hot, in_row, preferred_element_type=F32)
    same = day(0, (size, LANES), 0) == iota((size, LANES), 1) % days
    in_out[:, :LANES] = jnp.where(same, wide, 0.0).astype(BF)
    same = day(0, (size, days), 0) == iota((size, days), 1)
    b_high, b_low = halves(column[:, layers : layers + 1])
    for at, part in ((LANES, b_high), (LANES + days, b_low)):
        in_out[:, at : at + days] = jnp.where(
            same, jnp.broadcast_to(part.astype(F32), (size, days)), 0.0
        ).astype(BF)
    out_row = nt(jnp.broadcast_to(out_ref[...], (8, channels)), hot)
    same = iota((days, size), 0) == day(0, (days, size), 1)
    out_out[...] = jnp.where(same, jnp.broadcast_to(out_row[0:1], (days, size)), 0.0).astype(BF)

    bands, tiles = lax.axis_size("day"), lax.axis_size("tile")
    band_at, tile_at = lax.axis_index("day"), lax.axis_index("tile")
    cols, rows = width - 2 * HALO, 16
    for b in range(valid_out.shape[0]):
        row, q = place_of(b, width, (1, LANES))
        low_r = jnp.where(band_at == 0, HALO, 0)
        high_r = jnp.where(band_at == bands - 1, rows + HALO, rows + 2 * HALO)
        low_q = jnp.where(tile_at == 0, HALO, 0)
        high_q = jnp.where(tile_at == tiles - 1, cols + HALO, cols + 2 * HALO)
        inside = (row >= low_r) & (row < high_r) & (q >= low_q) & (q < high_q)
        valid_out[b : b + 1] = jnp.where(inside, 1.0, 0.0)


def main_kernel(
    sources,
    land_ref,
    land_left_ref,
    land_right_ref,
    own_land_ref,
    out_b_ref,
    *refs,
):
    given, out_ref, x_ref, v_ref, y_ref, bias_ref = refs[:8], refs[8], refs[9], refs[10], refs[11], refs[12]
    held, taps_sem, sem = refs[13:21], refs[21], refs[22]
    arrived_ref, banded_ref, first_ref, rest_ref, column_ref, in_ref, out_w_ref, valid_ref = held
    names = ("arrived", "banded", "first", "rest", "column", "in", "out", "valid")
    copies = {
        name: pltpu.make_async_copy(a, b, sem.at[i])
        for i, (name, a, b) in enumerate(zip(names, given, held))
        if name != "banded"
    }
    for name in ("arrived", "in", "column", "first", "valid", "rest", "out"):
        copies[name].start()
    fetch = [
        pltpu.make_async_copy(given[1].at[l], banded_ref.at[l], taps_sem.at[l]) for l in range(banded_ref.shape[0])
    ]
    channels = banded_ref.shape[1]
    layers = banded_ref.shape[0]
    width = LANES + 2 * HALO
    rows_in = 24

    lane = iota((LANES, LANES), 1)

    def expand(b):
        row, q = place_of(b, width, (LANES, LANES))
        side = jnp.where(q < HALO, 1, jnp.where(q >= LANES + HALO, 2, 0))
        return jnp.where((24 * side + row == iota((LANES, LANES), 0)) & (row < rows_in), 1.0, 0.0).astype(BF)

    copies["arrived"].wait()
    tail = arrived_ref[:, 96:104, :].astype(F32).reshape(8 * sources, LANES).astype(BF)
    pick_r, pick_c = iota((7 * sources, 8 * sources), 0), iota((7 * sources, 8 * sources), 1)
    pick = ((pick_c // 8 == pick_r % sources) & (pick_c % 8 == pick_r // sources)).astype(F32).astype(BF)
    parts = jnp.dot(pick, tail, preferred_element_type=F32).astype(BF)
    side_rows = [parts[j * sources : (j + 1) * sources] for j in range(6)]
    meta = parts[6 * sources :]
    wanted = (iota((16, LANES), 1) == iota((16, LANES), 0) + 72).astype(F32).astype(BF)
    tag_rows = lax.dot_general(wanted, meta, (((1,), (1,)), ((), ())), preferred_element_type=F32)
    repeat = (iota((sources, 8 * sources), 1) // 8 == iota((sources, 8 * sources), 0)).astype(F32).astype(BF)
    tag_wide = jnp.dot(tag_rows.astype(BF), repeat, preferred_element_type=F32)
    m, k = iota((256, 8 * sources), 0), iota((256, 8 * sources), 1)
    same = m // 32 == k % 8
    day_of = (m % 32 + 1).astype(F32)
    perms = [
        jnp.where(same & (tag_wide[b : b + 1] == day_of), 1.0, 0.0).astype(BF) for b in range(3)
    ]
    day_col = (iota((32, sources), 0) + 1).astype(F32)
    hot = [jnp.where(tag_rows[i : i + 1] == day_col, 1.0, 0.0).astype(BF) for i in range(9)]

    lane32 = iota((32, LANES), 1)
    cover = jnp.zeros((32, LANES), F32)
    for side in range(3):
        for band, (lo, hi) in enumerate(((0, 4), (4, 20), (20, 24))):
            got = jnp.dot(hot[3 * side + band], meta, preferred_element_type=F32)
            here = (lane32 >= 24 * side + lo) & (lane32 < 24 * side + hi)
            cover = jnp.where(here, got, cover)
    cover = cover.astype(BF)

    packed = [[None] * 2 for _ in range(4)]
    for j in range(6):
        band = 0 if j == 0 else (2 if j == 5 else 1)
        left = jnp.dot(hot[3 + band], side_rows[j], preferred_element_type=F32)
        right = jnp.dot(hot[6 + band], side_rows[j], preferred_element_type=F32)
        both = jnp.where(lane32 % 8 < 4, left, right)
        half, start = (32 * j) // LANES, (32 * j) % LANES
        here = (lane32 >= start) & (lane32 < start + 32)
        for v in range(4):
            moved = pltpu.roll(both, (start - 32 * v) % LANES, 1)
            had = packed[v][half]
            packed[v][half] = jnp.where(here, moved, 0.0 if had is None else had)
    edges = [jnp.concatenate([packed[v][h] for v in range(4)], 0) for h in range(2)]

    rolled = []
    pairs = []
    for p in range(0, 12, 2):
        band = 0 if p < 2 else (2 if p >= 10 else 1)
        rows = [
            arrived_ref[:, 8 * i : 8 * i + 8, :].astype(F32).reshape(8 * sources, LANES).astype(BF)
            for i in (p, p + 1)
        ]
        both = jnp.dot(perms[band], jnp.concatenate(rows, 1), preferred_element_type=F32)
        pairs += [both[:, :LANES], both[:, LANES:]]
    for p, got in enumerate(pairs):
        for r2 in range(2):
            row = 2 * p + r2
            rolled.append(pltpu.roll(got[128 * r2 : 128 * r2 + 128], (8 * row + 4) % LANES, 1))
    zero = jnp.zeros((LANES, LANES), F32)

    def flat_block(b):
        now, start = (b, 8 * b + 4) if b <= 15 else ((b - 1, 8 * b - 132) if b >= 17 else (16, 132))
        before = now - 1
        now_v = rolled[now] if now < rows_in else zero
        before_v = rolled[before] if before >= 0 else zero
        edge = edges[0] if b <= 16 else edges[1]
        return jnp.where(lane < start - 8, before_v, jnp.where(lane < start, edge, now_v))

    land, land_left, land_right = (
        pltpu.roll(
            jnp.concatenate([ref[...].astype(F32), jnp.zeros((LANES - rows_in, LANES), F32)], 0), 4, 1, stride=8, stride_axis=0
        )
        for ref in (land_ref, land_left_ref, land_right_ref)
    )
    lane1 = iota((1, LANES), 1)

    def land_block(b):
        now, start = (b, 8 * b + 4) if b <= 15 else ((b - 1, 8 * b - 132) if b >= 17 else (16, 132))
        pick = lambda a, r: a[r : r + 1] if 0 <= r < rows_in else jnp.zeros((1, LANES), F32)
        value = jnp.where(lane1 < start - 4, pick(land_right, now - 1), pick(land_left, now))
        value = jnp.where(lane1 < start - 8, pick(land, now - 1), value)
        return jnp.where(lane1 < start, value, pick(land, now))

    copies["in"].wait()
    for copy in fetch:
        copy.start()
    for j in range(13):
        pair = []
        for b in (2 * j, 2 * j + 1):
            keep = jnp.dot(cover, expand(b), preferred_element_type=F32)
            pair.append((jnp.concatenate([flat_block(b), keep, keep], 0) * land_block(b)).astype(BF))
        got = jnp.dot(in_ref[...], jnp.concatenate(pair, 1), preferred_element_type=F32).astype(BF)
        x_ref[2 * j] = got[:, :LANES]
        x_ref[2 * j + 1] = got[:, LANES:]

    for name in ("column", "first", "valid"):
        copies[name].wait()
    for l in range(layers):
        bias_ref[l] = jnp.broadcast_to(column_ref[:, l : l + 1], bias_ref.shape[1:])
    for b in (0, 1, 28, 29):
        v_ref[b] = jnp.zeros(v_ref.shape[1:], BF)

    def mix(l, b):
        both = jnp.concatenate([x_ref[b], x_ref[b + 1]], 1)
        ok = jnp.concatenate([valid_ref[b : b + 1], valid_ref[b + 1 : b + 2]], 1)
        bias = bias_ref[l]
        for p in range(2):
            half = slice(256 * p, 256 * p + 256)
            if l == 0:
                acc = jnp.dot(first_ref[half], both, preferred_element_type=F32)
            else:
                acc = jnp.dot(rest_ref[l - 1], both[half], preferred_element_type=F32)
            h = acc + jnp.concatenate([bias[half], bias[half]], 1)
            v = ((h + h * jnp.tanh(h)) * ok).astype(BF)
            v_ref[b + 2, half] = v[:, :LANES]
            v_ref[b + 3, half] = v[:, LANES:]

    def stencil(l, starts, c):
        groups = [slice(c * 16 + 256 * p, c * 16 + 256 * p + 16) for p in range(2)]
        lhs = jnp.concatenate(
            [
                jnp.concatenate([v_ref[b + i, rows] for i in range(6)], 1)
                for b in starts
                for rows in groups
            ],
            0,
        )
        t = [jnp.zeros((LANES, LANES), BF)] + [banded_ref[l, c, i] for i in range(5)]
        t = t + [t[0]]
        rhs = jnp.concatenate([jnp.concatenate([t[a + 1], t[a]], 1) for a in range(6)], 0)
        acc = jnp.dot(lhs, rhs, preferred_element_type=F32)
        at = 0
        for b in starts:
            for rows in groups:
                for h in range(2):
                    part = acc[at : at + 16, LANES * h : LANES * h + LANES]
                    x_ref[b + h, rows] = (x_ref[b + h, rows].astype(F32) + part).astype(BF)
                at += 16

    for l in range(layers):
        pairs_v, pairs_x = (
            range(low * width // LANES, -(-(rows_in - low) * width // LANES), 2) for low in (l, l + 1)
        )
        if l == 1:
            copies["rest"].wait()
        for b in pairs_v:
            mix(l, b)
        fetch[l].wait()
        for c in range(channels):
            stencil(l, pairs_x, c)

    copies["out"].wait()
    for j in range(2, 11):
        got = jnp.dot(
            out_w_ref[...], jnp.concatenate([x_ref[2 * j], x_ref[2 * j + 1]], 1), preferred_element_type=F32
        )
        y_ref[2 * j] = got[:, :LANES]
        y_ref[2 * j + 1] = got[:, LANES:]
    lane_d = iota((32, LANES), 1)
    for r in range(16):
        block, start = divmod((r + HALO) * width + HALO, LANES)
        back = (LANES - start) % LANES
        value = pltpu.roll(y_ref[block], back, 1) if back else y_ref[block]
        if start:
            value = jnp.where(lane_d < LANES - start, value, pltpu.roll(y_ref[block + 1], back, 1))
        out_ref[:, r, :] = (value + out_b_ref[0]) * own_land_ref[r : r + 1].astype(F32)


def local(
    scene_rows,
    granule_list,
    land_mask,
    in_weight,
    obs_bias,
    time_taps,
    mix_weight,
    mix_bias,
    space_taps,
    out_weight,
    out_bias,
):
    bands = lax.axis_size("day")
    tiles = lax.axis_size("tile")
    days_here = granule_list.shape[0]
    days = days_here * bands
    rows, cols = land_mask.shape
    channels, variables = in_weight.shape
    layers = mix_weight.shape[0]
    sources = bands * tiles
    width = cols + 2 * HALO
    slots = scene_rows.shape[3]
    n_block = 26

    notes = jnp.transpose(granule_list.reshape(days_here, bands, 3), (2, 1, 0))
    granules = days_here * bands
    outgoing = pl.pallas_call(
        functools.partial(pack_kernel, tiles, bands, days_here),
        out_shape=jax.ShapeDtypeStruct((sources, 104, cols), BF),
        in_specs=[HBM, SMEM],
        out_specs=VMEM,
        scratch_shapes=[
            pltpu.VMEM((variables, slots, cols), BF),
            pltpu.VMEM((variables, slots + 32, cols), F32),
            pltpu.VMEM((bands, 64, cols), F32),
            pltpu.VMEM((granules, 64, cols), BF),
            pltpu.VMEM((granules, 8, cols), F32),
            pltpu.VMEM(((bands + 2) * (tiles + 2), 8, cols), F32),
            pltpu.SemaphoreType.DMA((variables,)),
        ],
        compiler_params=pltpu.CompilerParams(vmem_limit_bytes=60 * 2**20),
        name="pack",
    )(scene_rows.reshape(variables, slots, cols), notes)

    size = channels * days
    shape = lambda *dims, dtype=BF: jax.ShapeDtypeStruct(dims, dtype)
    land_mask, time_taps, outgoing = lax.optimization_barrier((land_mask, time_taps, outgoing))
    params = (
        jnp.transpose(space_taps, (2, 0, 1)),
        jnp.transpose(time_taps, (2, 0, 1)),
        mix_weight,
        mix_bias,
        in_weight.T,
        obs_bias.reshape(1, channels),
        out_weight.reshape(1, channels),
    )
    made = (
        shape(layers, channels, 5, LANES, LANES),
        shape(size, size),
        shape(layers - 1, size // 2, size // 2),
        shape(size, LANES, dtype=F32),
        shape(size, (variables + 2) * days),
        shape(days, size),
        shape(n_block, LANES, dtype=F32),
    )
    weights = pl.pallas_call(
        functools.partial(weights_kernel, width),
        out_shape=made,
        in_specs=[HBM] * 7,
        out_specs=(HBM,) * 7,
        scratch_shapes=[pltpu.SMEM(params[0].shape, F32)]
        + [pltpu.VMEM(a.shape, a.dtype) for a in params[1:]]
        + [pltpu.VMEM(a.shape, a.dtype) for a in made]
        + [pltpu.SemaphoreType.DMA((8,))],
        compiler_params=pltpu.CompilerParams(vmem_limit_bytes=60 * 2**20),
        cost_estimate=pl.CostEstimate(flops=2 * 10**9, bytes_accessed=24 * 2**20, transcendentals=0),
        name="weights",
    )(*params)
    arrived = lax.all_to_all(outgoing, ("day", "tile"), split_axis=0, concat_axis=0, tiled=True)

    forward = lambda n: [(i, i + 1) for i in range(n - 1)]
    backward = lambda n: [(i + 1, i) for i in range(n - 1)]
    land = land_mask.astype(BF)
    land = jnp.concatenate(
        [
            lax.ppermute(land[rows - HALO :], "day", forward(bands)),
            land,
            lax.ppermute(land[:HALO], "day", backward(bands)),
        ],
        0,
    )
    land_left = lax.ppermute(land, "tile", forward(tiles))
    land_right = lax.ppermute(land, "tile", backward(tiles))

    return pl.pallas_call(
        functools.partial(main_kernel, sources),
        out_shape=jax.ShapeDtypeStruct((days, rows, cols), F32),
        in_specs=[VMEM] * 4 + [SMEM] + [HBM] * 8,
        out_specs=VMEM,
        scratch_shapes=[
            pltpu.VMEM((n_block, channels * days, LANES), BF),
            pltpu.VMEM((n_block + 4, channels * days, LANES), BF),
            pltpu.VMEM((n_block, days, LANES), F32),
            pltpu.VMEM((layers, size, LANES), F32),
            pltpu.VMEM(arrived.shape, BF),
        ]
        + [pltpu.VMEM(a.shape, a.dtype) for a in made]
        + [pltpu.SemaphoreType.DMA((layers,)), pltpu.SemaphoreType.DMA((8,))],
        compiler_params=pltpu.CompilerParams(vmem_limit_bytes=60 * 2**20),
        name="blocks",
    )(
        land,
        land_left,
        land_right,
        land_mask,
        out_bias,
        arrived,
        *weights,
    )


def solution(mesh):
    placed = (
        P(None, "day", "tile", None, None),
        P("day", "tile", None, None),
        P("day", "tile"),
        P(),
        P(),
        P(),
        P(),
        P(),
        P(),
        P(),
        P(),
    )
    return jax.shard_map(
        local, mesh=mesh, in_specs=placed, out_specs=P(None, "day", "tile"), check_vma=False
    )
```

```python
import functools

import jax
import jax.numpy as jnp
from jax import lax
from jax.experimental import pallas as pl
from jax.experimental.pallas import tpu as pltpu
from jax.sharding import PartitionSpec as P

BF = jnp.bfloat16
F32 = jnp.float32
HALO = 4
LANES = 128
VMEM = pl.BlockSpec(memory_space=pltpu.VMEM)
SMEM = pl.BlockSpec(memory_space=pltpu.SMEM)
HBM = pl.BlockSpec(memory_space=pltpu.HBM)


def iota(shape, dim):
    return lax.broadcasted_iota(jnp.int32, shape, dim)


def pack_kernel(tiles, bands, days, scene_ref, list_ref, out_ref, scene, wide, mixed, blocks, picked, tail, sem):
    variables, slots = scene_ref.shape[0], scene_ref.shape[1]
    copies = [pltpu.make_async_copy(scene_ref.at[v], scene.at[v], sem.at[v]) for v in range(variables)]
    for copy in copies:
        copy.start()

    def clear(i, c):
        out_ref[i] = jnp.zeros(out_ref.shape[1:], BF)
        return c

    lax.fori_loop(0, out_ref.shape[0], clear, 0)

    def clear_tail(i, c):
        tail[i] = jnp.zeros((8, LANES), F32)
        return c

    lax.fori_loop(0, tail.shape[0], clear_tail, 0)
    for v in range(variables):
        wide[v, 0:16] = jnp.zeros((16, LANES), F32)
        copies[v].wait()
        wide[v, 16 : 16 + slots] = scene[v].astype(F32)
        wide[v, 16 + slots : 32 + slots] = jnp.zeros((16, LANES), F32)
    row = iota((16, LANES), 0)

    def place(day, first):
        for band in range(bands):
            tile, offset, count = (list_ref[k, band, day] for k in range(3))
            live = (row >= offset) & (row < offset + count)
            for v in range(variables):
                rows = wide[v, pl.ds(16 + first - offset, 16), :]
                mixed[band, pl.ds(v, 16, stride=4), :] = jnp.where(live, rows, 0.0)
            block = mixed[band].astype(BF)
            blocks[day * bands + band] = block
            out_ref[band * tiles + tile, 16:80] = block
            if band + 1 < bands:
                out_ref[(band + 1) * tiles + tile, 0:16] = block[48:64]
            if band > 0:
                out_ref[(band - 1) * tiles + tile, 80:96] = block[0:16]
            first = first + count
        return first

    lax.fori_loop(0, days, place, jnp.int32(0))

    q, lane = iota((LANES, LANES), 0), iota((LANES, LANES), 1)
    edge = lane % 8
    choose = (q == jnp.where(edge < 4, 124 + edge, edge - 4)).astype(F32).astype(BF)
    granules = days * bands
    spread = jnp.dot(
        blocks[...].reshape(granules * 64, LANES), choose, preferred_element_type=F32
    ).reshape(granules, 64, LANES)
    r64, l64 = iota((64, LANES), 0), iota((64, LANES), 1)
    own = (r64 % 4 == l64 // 32) & ((r64 // 4) % 4 == (l64 % 32) // 8)
    for g in range(granules):
        kept = jnp.where(own, spread[g], 0.0)
        part = [jnp.sum(kept[16 * j : 16 * j + 16], axis=0, keepdims=True) for j in range(4)]
        zero = jnp.zeros((2, LANES), F32)
        picked[g] = jnp.concatenate([part[3], part[0], part[1], part[2], part[3], part[0], zero], 0)

    sub, col = iota((8, LANES), 0), iota((8, LANES), 1)
    row_of = {0: (sub >= 1) & (sub <= 4), 1: sub == 0, -1: sub == 5}
    is_left = col % 8 < 4
    day_base = lax.axis_index("day") * days

    def tags(day, c):
        for band in range(bands):
            tile, offset, count = (list_ref[k, band, day] for k in range(3))
            sides = picked[day * bands + band]
            for step, shift, low, high, region in ((0, 4, 0, 16, 1), (1, -12, 12, 16, 0), (-1, 20, 0, 4, 2)):
                lo, hi = jnp.maximum(offset, low), jnp.minimum(offset + count, high)
                for side in range(3):
                    r = col - (24 * side + shift)
                    tag = jnp.where(col == 72 + 3 * side + region, (day_base + day + 1).astype(F32), 0.0)
                    note = jnp.where(sub == 6, jnp.where((r >= lo) & (r < hi), 1.0, tag), 0.0)
                    if side > 0:
                        wanted = row_of[step] & (is_left if side == 1 else jnp.logical_not(is_left))
                        note = note + jnp.where(wanted, sides, 0.0)
                    at = (band + step + 1) * (tiles + 2) + tile + (1, 2, 0)[side]
                    tail[at] = tail[at] + note
        return c

    lax.fori_loop(0, days, tags, 0)
    for band in range(bands):

        def finish(tile, c, band=band):
            out_ref[band * tiles + tile, 96:104] = tail[(band + 1) * (tiles + 2) + tile + 1].astype(BF)
            return c

        lax.fori_loop(0, tiles, finish, 0)


def halves(value):
    high = value.astype(BF)
    return high, (value - high.astype(F32)).astype(BF)


def place_of(block, width, shape):
    first = block * LANES // width
    lane = iota(shape, len(shape) - 1)
    row = first + (lane >= (first + 1) * width - block * LANES).astype(jnp.int32)
    return row, lane + block * LANES - row * width


def weights_kernel(
    width,
    *refs,
):
    params, results, held, made, sem = refs[:7], refs[7:14], refs[14:21], refs[21:28], refs[28]
    copies = [pltpu.make_async_copy(a, b, sem.at[i]) for i, (a, b) in enumerate(zip(params, held))]
    for copy in copies:
        copy.start()
    for copy in copies:
        copy.wait()
    weights_body(width, *held, *made)
    copies = [pltpu.make_async_copy(a, b, sem.at[i]) for i, (a, b) in enumerate(zip(made, results))]
    for copy in copies:
        copy.start()
    for copy in copies:
        copy.wait()


def weights_body(
    width,
    taps_ref,
    time_ref,
    mix_ref,
    mix_bias_ref,
    in_ref,
    obs_bias_ref,
    out_ref,
    band_out,
    first_out,
    rest_out,
    bias_out,
    in_out,
    out_out,
    valid_out,
):
    layers, channels = mix_ref.shape[0], mix_ref.shape[1]
    half = first_out.shape[0] // (2 * channels)
    days = 2 * half
    size = channels * days

    delta = [(k // 3 - 1) * width + k % 3 - 1 for k in range(9)]
    offset = iota((16, LANES), 0) - iota((16, LANES), 1)

    def band(at, c):
        l, ch = at // channels, at % channels
        taps = [taps_ref[k, l, ch] for k in range(9)]
        for t in range(5):
            for k0 in range(0, LANES, 16):
                value = jnp.zeros((16, LANES), F32)
                for tap, d in zip(taps, delta):
                    want = d - LANES * (t - 2) - k0
                    if -(LANES - 1) <= want <= 15:
                        value = jnp.where(offset == want, tap, value)
                band_out[l, ch, t, k0 : k0 + 16] = value.astype(BF)
        return c

    lax.fori_loop(0, layers * channels, band, 0)

    hot = ((iota((size, channels), 0) // half) % channels == iota((size, channels), 1)).astype(F32).astype(BF)
    day = lambda n, shape, dim: 2 * (iota(shape, dim) % half) + iota(shape, dim) // (channels * half)

    def widened(l, k, count):
        mixed = (0.5 * mix_ref[l].astype(F32) * time_ref[k, l : l + 1]).astype(BF)
        rows = jnp.dot(hot[:count], mixed, preferred_element_type=F32).astype(BF)
        return lax.dot_general(rows, hot[:count], (((1,), (1,)), ((), ())), preferred_element_type=F32)

    for l in range(layers):
        count = size if l == 0 else size // 2
        gap = day(l, (count, count), 1) - day(l, (count, count), 0)
        value = jnp.zeros((count, count), F32)
        for k in range(3):
            value = jnp.where(gap == (k - 1) * 2**l, widened(l, k, count), value)
        if l == 0:
            first_out[...] = value.astype(BF)
        else:
            rest_out[l - 1] = value.astype(BF)

    spare = jnp.zeros((LANES - layers - 1, channels), F32)
    rows8 = jnp.concatenate([0.5 * mix_bias_ref[...], obs_bias_ref[...], spare], 0)
    high, rest = halves(rows8)
    mid, low = halves(rows8 - high.astype(F32))
    nt = lambda a, b: lax.dot_general(a, b, (((1,), (1,)), ((), ())), preferred_element_type=F32)
    column = nt(hot, high) + (nt(hot, mid) + nt(hot, low))
    bias_out[...] = column

    variables = in_ref.shape[0]
    repeat = (iota((variables, LANES), 1) // days == iota((variables, LANES), 0)).astype(F32).astype(BF)
    in_row = lax.dot_general(
        in_ref[...].astype(F32), repeat.astype(F32), (((0,), (0,)), ((), ())), preferred_element_type=F32
    ).astype(BF)
    wide = jnp.dot(hot, in_row, preferred_element_type=F32)
    same = day(0, (size, LANES), 0) == iota((size, LANES), 1) % days
    in_out[:, :LANES] = jnp.where(same, wide, 0.0).astype(BF)
    same = day(0, (size, days), 0) == iota((size, days), 1)
    b_high, b_low = halves(column[:, layers : layers + 1])
    for at, part in ((LANES, b_high), (LANES + days, b_low)):
        in_out[:, at : at + days] = jnp.where(
            same, jnp.broadcast_to(part.astype(F32), (size, days)), 0.0
        ).astype(BF)
    out_row = nt(jnp.broadcast_to(out_ref[...], (8, channels)), hot)
    same = iota((days, size), 0) == day(0, (days, size), 1)
    out_out[...] = jnp.where(same, jnp.broadcast_to(out_row[0:1], (days, size)), 0.0).astype(BF)

    bands, tiles = lax.axis_size("day"), lax.axis_size("tile")
    band_at, tile_at = lax.axis_index("day"), lax.axis_index("tile")
    cols, rows = width - 2 * HALO, 16
    for b in range(valid_out.shape[0]):
        row, q = place_of(b, width, (1, LANES))
        low_r = jnp.where(band_at == 0, HALO, 0)
        high_r = jnp.where(band_at == bands - 1, rows + HALO, rows + 2 * HALO)
        low_q = jnp.where(tile_at == 0, HALO, 0)
        high_q = jnp.where(tile_at == tiles - 1, cols + HALO, cols + 2 * HALO)
        inside = (row >= low_r) & (row < high_r) & (q >= low_q) & (q < high_q)
        valid_out[b : b + 1] = jnp.where(inside, 1.0, 0.0)


def main_kernel(
    sources,
    out_b_ref,
    *refs,
):
    given, out_ref, x_ref, v_ref, y_ref, bias_ref = refs[:12], refs[12], refs[13], refs[14], refs[15], refs[16]
    held, taps_sem, sem = refs[17:29], refs[29], refs[30]
    names = ("arrived", "land", "left", "right", "own", "banded", "first", "rest", "column", "in", "out", "valid")
    arrived_ref, land_ref, land_left_ref, land_right_ref, own_land_ref = held[:5]
    banded_ref, first_ref, rest_ref, column_ref, in_ref, out_w_ref, valid_ref = held[5:]
    copies = {
        name: pltpu.make_async_copy(a, b, sem.at[i])
        for i, (name, a, b) in enumerate(zip(names, given, held))
        if name != "banded"
    }
    for name in ("arrived", "land", "left", "right", "in", "column", "first", "valid", "rest", "out", "own"):
        copies[name].start()
    fetch = [
        pltpu.make_async_copy(given[5].at[l], banded_ref.at[l], taps_sem.at[l]) for l in range(banded_ref.shape[0])
    ]
    channels = banded_ref.shape[1]
    layers = banded_ref.shape[0]
    width = LANES + 2 * HALO
    rows_in = 24

    lane = iota((LANES, LANES), 1)

    def expand(b):
        row, q = place_of(b, width, (LANES, LANES))
        side = jnp.where(q < HALO, 1, jnp.where(q >= LANES + HALO, 2, 0))
        return jnp.where((24 * side + row == iota((LANES, LANES), 0)) & (row < rows_in), 1.0, 0.0).astype(BF)

    copies["arrived"].wait()
    tail = arrived_ref[:, 96:104, :].astype(F32).reshape(8 * sources, LANES).astype(BF)
    pick_r, pick_c = iota((7 * sources, 8 * sources), 0), iota((7 * sources, 8 * sources), 1)
    pick = ((pick_c // 8 == pick_r % sources) & (pick_c % 8 == pick_r // sources)).astype(F32).astype(BF)
    parts = jnp.dot(pick, tail, preferred_element_type=F32).astype(BF)
    side_rows = [parts[j * sources : (j + 1) * sources] for j in range(6)]
    meta = parts[6 * sources :]
    wanted = (iota((16, LANES), 1) == iota((16, LANES), 0) + 72).astype(F32).astype(BF)
    tag_rows = lax.dot_general(wanted, meta, (((1,), (1,)), ((), ())), preferred_element_type=F32)
    repeat = (iota((sources, 8 * sources), 1) // 8 == iota((sources, 8 * sources), 0)).astype(F32).astype(BF)
    tag_wide = jnp.dot(tag_rows.astype(BF), repeat, preferred_element_type=F32)
    m, k = iota((256, 8 * sources), 0), iota((256, 8 * sources), 1)
    same = m // 32 == k % 8
    day_of = (m % 32 + 1).astype(F32)
    perms = [
        jnp.where(same & (tag_wide[b : b + 1] == day_of), 1.0, 0.0).astype(BF) for b in range(3)
    ]
    day_col = (iota((32, sources), 0) + 1).astype(F32)
    hot = [jnp.where(tag_rows[i : i + 1] == day_col, 1.0, 0.0).astype(BF) for i in range(9)]

    lane32 = iota((32, LANES), 1)
    cover = jnp.zeros((32, LANES), F32)
    for side in range(3):
        for band, (lo, hi) in enumerate(((0, 4), (4, 20), (20, 24))):
            got = jnp.dot(hot[3 * side + band], meta, preferred_element_type=F32)
            here = (lane32 >= 24 * side + lo) & (lane32 < 24 * side + hi)
            cover = jnp.where(here, got, cover)
    cover = cover.astype(BF)

    packed = [[None] * 2 for _ in range(4)]
    for j in range(6):
        band = 0 if j == 0 else (2 if j == 5 else 1)
        left = jnp.dot(hot[3 + band], side_rows[j], preferred_element_type=F32)
        right = jnp.dot(hot[6 + band], side_rows[j], preferred_element_type=F32)
        both = jnp.where(lane32 % 8 < 4, left, right)
        half, start = (32 * j) // LANES, (32 * j) % LANES
        here = (lane32 >= start) & (lane32 < start + 32)
        for v in range(4):
            moved = pltpu.roll(both, (start - 32 * v) % LANES, 1)
            had = packed[v][half]
            packed[v][half] = jnp.where(here, moved, 0.0 if had is None else had)
    edges = [jnp.concatenate([packed[v][h] for v in range(4)], 0) for h in range(2)]

    rolled = []
    pairs = []
    for p in range(0, 12, 2):
        band = 0 if p < 2 else (2 if p >= 10 else 1)
        rows = [
            arrived_ref[:, 8 * i : 8 * i + 8, :].astype(F32).reshape(8 * sources, LANES).astype(BF)
            for i in (p, p + 1)
        ]
        both = jnp.dot(perms[band], jnp.concatenate(rows, 1), preferred_element_type=F32)
        pairs += [both[:, :LANES], both[:, LANES:]]
    for p, got in enumerate(pairs):
        for r2 in range(2):
            row = 2 * p + r2
            rolled.append(pltpu.roll(got[128 * r2 : 128 * r2 + 128], (8 * row + 4) % LANES, 1))
    zero = jnp.zeros((LANES, LANES), F32)

    def flat_block(b):
        now, start = (b, 8 * b + 4) if b <= 15 else ((b - 1, 8 * b - 132) if b >= 17 else (16, 132))
        before = now - 1
        now_v = rolled[now] if now < rows_in else zero
        before_v = rolled[before] if before >= 0 else zero
        edge = edges[0] if b <= 16 else edges[1]
        return jnp.where(lane < start - 8, before_v, jnp.where(lane < start, edge, now_v))

    for name in ("land", "left", "right"):
        copies[name].wait()
    land, land_left, land_right = (
        pltpu.roll(
            jnp.concatenate([ref[...].astype(F32), jnp.zeros((LANES - rows_in, LANES), F32)], 0), 4, 1, stride=8, stride_axis=0
        )
        for ref in (land_ref, land_left_ref, land_right_ref)
    )
    lane1 = iota((1, LANES), 1)

    def land_block(b):
        now, start = (b, 8 * b + 4) if b <= 15 else ((b - 1, 8 * b - 132) if b >= 17 else (16, 132))
        pick = lambda a, r: a[r : r + 1] if 0 <= r < rows_in else jnp.zeros((1, LANES), F32)
        value = jnp.where(lane1 < start - 4, pick(land_right, now - 1), pick(land_left, now))
        value = jnp.where(lane1 < start - 8, pick(land, now - 1), value)
        return jnp.where(lane1 < start, value, pick(land, now))

    copies["in"].wait()
    for copy in fetch:
        copy.start()
    for j in range(13):
        pair = []
        for b in (2 * j, 2 * j + 1):
            keep = jnp.dot(cover, expand(b), preferred_element_type=F32)
            pair.append((jnp.concatenate([flat_block(b), keep, keep], 0) * land_block(b)).astype(BF))
        got = jnp.dot(in_ref[...], jnp.concatenate(pair, 1), preferred_element_type=F32).astype(BF)
        x_ref[2 * j] = got[:, :LANES]
        x_ref[2 * j + 1] = got[:, LANES:]

    for name in ("column", "first", "valid"):
        copies[name].wait()
    for l in range(layers):
        bias_ref[l] = jnp.broadcast_to(column_ref[:, l : l + 1], bias_ref.shape[1:])
    for b in (0, 1, 28, 29):
        v_ref[b] = jnp.zeros(v_ref.shape[1:], BF)

    def mix(l, b):
        both = jnp.concatenate([x_ref[b], x_ref[b + 1]], 1)
        ok = jnp.concatenate([valid_ref[b : b + 1], valid_ref[b + 1 : b + 2]], 1)
        bias = bias_ref[l]
        for p in range(2):
            half = slice(256 * p, 256 * p + 256)
            if l == 0:
                acc = jnp.dot(first_ref[half], both, preferred_element_type=F32)
            else:
                acc = jnp.dot(rest_ref[l - 1], both[half], preferred_element_type=F32)
            h = acc + jnp.concatenate([bias[half], bias[half]], 1)
            v = ((h + h * jnp.tanh(h)) * ok).astype(BF)
            v_ref[b + 2, half] = v[:, :LANES]
            v_ref[b + 3, half] = v[:, LANES:]

    def stencil(l, starts, c):
        groups = [slice(c * 16 + 256 * p, c * 16 + 256 * p + 16) for p in range(2)]
        lhs = jnp.concatenate(
            [
                jnp.concatenate([v_ref[b + i, rows] for i in range(6)], 1)
                for b in starts
                for rows in groups
            ],
            0,
        )
        t = [jnp.zeros((LANES, LANES), BF)] + [banded_ref[l, c, i] for i in range(5)]
        t = t + [t[0]]
        rhs = jnp.concatenate([jnp.concatenate([t[a + 1], t[a]], 1) for a in range(6)], 0)
        acc = jnp.dot(lhs, rhs, preferred_element_type=F32)
        at = 0
        for b in starts:
            for rows in groups:
                for h in range(2):
                    part = acc[at : at + 16, LANES * h : LANES * h + LANES]
                    x_ref[b + h, rows] = (x_ref[b + h, rows].astype(F32) + part).astype(BF)
                at += 16

    for l in range(layers):
        pairs_v, pairs_x = (
            range(low * width // LANES, -(-(rows_in - low) * width // LANES), 2) for low in (l, l + 1)
        )
        if l == 1:
            copies["rest"].wait()
        for b in pairs_v:
            mix(l, b)
        fetch[l].wait()
        for c in range(channels):
            stencil(l, pairs_x, c)

    copies["out"].wait()
    copies["own"].wait()
    for j in range(2, 11):
        got = jnp.dot(
            out_w_ref[...], jnp.concatenate([x_ref[2 * j], x_ref[2 * j + 1]], 1), preferred_element_type=F32
        )
        y_ref[2 * j] = got[:, :LANES]
        y_ref[2 * j + 1] = got[:, LANES:]
    lane_d = iota((32, LANES), 1)
    for r in range(16):
        block, start = divmod((r + HALO) * width + HALO, LANES)
        back = (LANES - start) % LANES
        value = pltpu.roll(y_ref[block], back, 1) if back else y_ref[block]
        if start:
            value = jnp.where(lane_d < LANES - start, value, pltpu.roll(y_ref[block + 1], back, 1))
        out_ref[:, r, :] = (value + out_b_ref[0]) * own_land_ref[r : r + 1].astype(F32)


def local(
    scene_rows,
    granule_list,
    land_mask,
    in_weight,
    obs_bias,
    time_taps,
    mix_weight,
    mix_bias,
    space_taps,
    out_weight,
    out_bias,
):
    bands = lax.axis_size("day")
    tiles = lax.axis_size("tile")
    days_here = granule_list.shape[0]
    days = days_here * bands
    rows, cols = land_mask.shape
    channels, variables = in_weight.shape
    layers = mix_weight.shape[0]
    sources = bands * tiles
    width = cols + 2 * HALO
    slots = scene_rows.shape[3]
    n_block = 26

    notes = jnp.transpose(granule_list.reshape(days_here, bands, 3), (2, 1, 0))
    granules = days_here * bands
    outgoing = pl.pallas_call(
        functools.partial(pack_kernel, tiles, bands, days_here),
        out_shape=jax.ShapeDtypeStruct((sources, 104, cols), BF),
        in_specs=[HBM, SMEM],
        out_specs=VMEM,
        scratch_shapes=[
            pltpu.VMEM((variables, slots, cols), BF),
            pltpu.VMEM((variables, slots + 32, cols), F32),
            pltpu.VMEM((bands, 64, cols), F32),
            pltpu.VMEM((granules, 64, cols), BF),
            pltpu.VMEM((granules, 8, cols), F32),
            pltpu.VMEM(((bands + 2) * (tiles + 2), 8, cols), F32),
            pltpu.SemaphoreType.DMA((variables,)),
        ],
        compiler_params=pltpu.CompilerParams(vmem_limit_bytes=60 * 2**20),
        name="pack",
    )(scene_rows.reshape(variables, slots, cols), notes)

    size = channels * days
    shape = lambda *dims, dtype=BF: jax.ShapeDtypeStruct(dims, dtype)
    land_mask, time_taps, outgoing = lax.optimization_barrier((land_mask, time_taps, outgoing))
    params = (
        jnp.transpose(space_taps, (2, 0, 1)),
        jnp.transpose(time_taps, (2, 0, 1)),
        mix_weight,
        mix_bias,
        in_weight.T,
        obs_bias.reshape(1, channels),
        out_weight.reshape(1, channels),
    )
    made = (
        shape(layers, channels, 5, LANES, LANES),
        shape(size, size),
        shape(layers - 1, size // 2, size // 2),
        shape(size, LANES, dtype=F32),
        shape(size, (variables + 2) * days),
        shape(days, size),
        shape(n_block, LANES, dtype=F32),
    )
    weights = pl.pallas_call(
        functools.partial(weights_kernel, width),
        out_shape=made,
        in_specs=[HBM] * 7,
        out_specs=(HBM,) * 7,
        scratch_shapes=[pltpu.SMEM(params[0].shape, F32)]
        + [pltpu.VMEM(a.shape, a.dtype) for a in params[1:]]
        + [pltpu.VMEM(a.shape, a.dtype) for a in made]
        + [pltpu.SemaphoreType.DMA((8,))],
        compiler_params=pltpu.CompilerParams(vmem_limit_bytes=60 * 2**20),
        cost_estimate=pl.CostEstimate(flops=2 * 10**9, bytes_accessed=24 * 2**20, transcendentals=0),
        name="weights",
    )(*params)
    arrived = lax.all_to_all(outgoing, ("day", "tile"), split_axis=0, concat_axis=0, tiled=True)

    forward = lambda n: [(i, i + 1) for i in range(n - 1)]
    backward = lambda n: [(i + 1, i) for i in range(n - 1)]
    land = land_mask.astype(BF)
    land = jnp.concatenate(
        [
            lax.ppermute(land[rows - HALO :], "day", forward(bands)),
            land,
            lax.ppermute(land[:HALO], "day", backward(bands)),
        ],
        0,
    )
    land_left = lax.ppermute(land, "tile", forward(tiles))
    land_right = lax.ppermute(land, "tile", backward(tiles))

    return pl.pallas_call(
        functools.partial(main_kernel, sources),
        out_shape=jax.ShapeDtypeStruct((days, rows, cols), F32),
        in_specs=[SMEM] + [HBM] * 12,
        out_specs=VMEM,
        scratch_shapes=[
            pltpu.VMEM((n_block, channels * days, LANES), BF),
            pltpu.VMEM((n_block + 4, channels * days, LANES), BF),
            pltpu.VMEM((n_block, days, LANES), F32),
            pltpu.VMEM((layers, size, LANES), F32),
        ]
        + [pltpu.VMEM(a.shape, a.dtype) for a in (arrived, land, land_left, land_right, land_mask)]
        + [pltpu.VMEM(a.shape, a.dtype) for a in made]
        + [pltpu.SemaphoreType.DMA((layers,)), pltpu.SemaphoreType.DMA((12,))],
        compiler_params=pltpu.CompilerParams(vmem_limit_bytes=60 * 2**20),
        name="blocks",
    )(out_bias, arrived, land, land_left, land_right, land_mask, *weights)


def solution(mesh):
    placed = (
        P(None, "day", "tile", None, None),
        P("day", "tile", None, None),
        P("day", "tile"),
        P(),
        P(),
        P(),
        P(),
        P(),
        P(),
        P(),
        P(),
    )
    return jax.shard_map(
        local, mesh=mesh, in_specs=placed, out_specs=P(None, "day", "tile"), check_vma=False
    )
```

```python
import functools

import jax
import jax.numpy as jnp
from jax import lax
from jax.experimental import pallas as pl
from jax.experimental.pallas import tpu as pltpu
from jax.sharding import PartitionSpec as P

BF = jnp.bfloat16
F32 = jnp.float32
HALO = 4
LANES = 128
VMEM = pl.BlockSpec(memory_space=pltpu.VMEM)
SMEM = pl.BlockSpec(memory_space=pltpu.SMEM)
HBM = pl.BlockSpec(memory_space=pltpu.HBM)


def iota(shape, dim):
    return lax.broadcasted_iota(jnp.int32, shape, dim)


def pack_kernel(tiles, bands, days, scene_ref, list_ref, out_ref, scene, wide, mixed, blocks, picked, tail, sem):
    variables, slots = scene_ref.shape[0], scene_ref.shape[1]
    copies = [pltpu.make_async_copy(scene_ref.at[v], scene.at[v], sem.at[v]) for v in range(variables)]
    for copy in copies:
        copy.start()

    def clear(i, c):
        out_ref[i] = jnp.zeros(out_ref.shape[1:], BF)
        return c

    lax.fori_loop(0, out_ref.shape[0], clear, 0)

    def clear_tail(i, c):
        tail[i] = jnp.zeros((8, LANES), F32)
        return c

    lax.fori_loop(0, tail.shape[0], clear_tail, 0)
    for v in range(variables):
        wide[v, 0:16] = jnp.zeros((16, LANES), F32)
        copies[v].wait()
        wide[v, 16 : 16 + slots] = scene[v].astype(F32)
        wide[v, 16 + slots : 32 + slots] = jnp.zeros((16, LANES), F32)
    row = iota((16, LANES), 0)

    def place(day, first):
        for band in range(bands):
            tile, offset, count = (list_ref[k, band, day] for k in range(3))
            live = (row >= offset) & (row < offset + count)
            for v in range(variables):
                rows = wide[v, pl.ds(16 + first - offset, 16), :]
                mixed[band, pl.ds(v, 16, stride=4), :] = jnp.where(live, rows, 0.0)
            block = mixed[band, 0:64].astype(BF)
            blocks[day * bands + band] = block
            out_ref[band * tiles + tile, 16:80] = block
            if band + 1 < bands:
                out_ref[(band + 1) * tiles + tile, 0:16] = block[48:64]
            if band > 0:
                out_ref[(band - 1) * tiles + tile, 80:96] = block[0:16]
            first = first + count
        return first

    lax.fori_loop(0, days, place, jnp.int32(0))

    q, lane = iota((LANES, LANES), 0), iota((LANES, LANES), 1)
    edge = lane % 8
    choose = (q == jnp.where(edge < 4, 124 + edge, edge - 4)).astype(F32).astype(BF)
    granules = days * bands
    spread = jnp.dot(
        blocks[...].reshape(granules * 64, LANES), choose, preferred_element_type=F32
    ).reshape(granules, 64, LANES)
    r64, l64 = iota((64, LANES), 0), iota((64, LANES), 1)
    own = (r64 % 4 == l64 // 32) & ((r64 // 4) % 4 == (l64 % 32) // 8)
    for g in range(granules):
        kept = jnp.where(own, spread[g], 0.0)
        part = [jnp.sum(kept[16 * j : 16 * j + 16], axis=0, keepdims=True) for j in range(4)]
        zero = jnp.zeros((2, LANES), F32)
        picked[g] = jnp.concatenate([part[3], part[0], part[1], part[2], part[3], part[0], zero], 0)

    sub, col = iota((8, LANES), 0), iota((8, LANES), 1)
    row_of = {0: (sub >= 1) & (sub <= 4), 1: sub == 0, -1: sub == 5}
    is_left = col % 8 < 4
    day_base = lax.axis_index("day") * days

    def tags(day, c):
        for band in range(bands):
            tile, offset, count = (list_ref[k, band, day] for k in range(3))
            sides = picked[day * bands + band]
            for step, shift, low, high, region in ((0, 4, 0, 16, 1), (1, -12, 12, 16, 0), (-1, 20, 0, 4, 2)):
                lo, hi = jnp.maximum(offset, low), jnp.minimum(offset + count, high)
                for side in range(3):
                    r = col - (24 * side + shift)
                    tag = jnp.where(col == 72 + 3 * side + region, (day_base + day + 1).astype(F32), 0.0)
                    note = jnp.where(sub == 6, jnp.where((r >= lo) & (r < hi), 1.0, tag), 0.0)
                    if side > 0:
                        wanted = row_of[step] & (is_left if side == 1 else jnp.logical_not(is_left))
                        note = note + jnp.where(wanted, sides, 0.0)
                    at = (band + step + 1) * (tiles + 2) + tile + (1, 2, 0)[side]
                    tail[at] = tail[at] + note
        return c

    lax.fori_loop(0, days, tags, 0)
    for band in range(bands):

        def finish(tile, c, band=band):
            out_ref[band * tiles + tile, 96:104] = tail[(band + 1) * (tiles + 2) + tile + 1].astype(BF)
            return c

        lax.fori_loop(0, tiles, finish, 0)


def halves(value):
    high = value.astype(BF)
    return high, (value - high.astype(F32)).astype(BF)


def place_of(block, width, shape):
    first = block * LANES // width
    lane = iota(shape, len(shape) - 1)
    row = first + (lane >= (first + 1) * width - block * LANES).astype(jnp.int32)
    return row, lane + block * LANES - row * width


def weights_kernel(
    width,
    *refs,
):
    params, results, held, made, sem = refs[:7], refs[7:14], refs[14:21], refs[21:28], refs[28]
    copies = [pltpu.make_async_copy(a, b, sem.at[i]) for i, (a, b) in enumerate(zip(params, held))]
    for copy in copies:
        copy.start()
    for copy in copies:
        copy.wait()
    weights_body(width, *held, *made)
    copies = [pltpu.make_async_copy(a, b, sem.at[i]) for i, (a, b) in enumerate(zip(made, results))]
    for copy in copies:
        copy.start()
    for copy in copies:
        copy.wait()


def weights_body(
    width,
    taps_ref,
    time_ref,
    mix_ref,
    mix_bias_ref,
    in_ref,
    obs_bias_ref,
    out_ref,
    band_out,
    first_out,
    rest_out,
    bias_out,
    in_out,
    out_out,
    valid_out,
):
    layers, channels = mix_ref.shape[0], mix_ref.shape[1]
    half = first_out.shape[0] // (2 * channels)
    days = 2 * half
    size = channels * days

    delta = [(k // 3 - 1) * width + k % 3 - 1 for k in range(9)]
    offset = iota((16, LANES), 0) - iota((16, LANES), 1)

    def band(at, c):
        l, ch = at // channels, at % channels
        taps = [taps_ref[k, l, ch] for k in range(9)]
        for t in range(5):
            for k0 in range(0, LANES, 16):
                value = jnp.zeros((16, LANES), F32)
                for tap, d in zip(taps, delta):
                    want = d - LANES * (t - 2) - k0
                    if -(LANES - 1) <= want <= 15:
                        value = jnp.where(offset == want, tap, value)
                band_out[l, ch, t, k0 : k0 + 16] = value.astype(BF)
        return c

    lax.fori_loop(0, layers * channels, band, 0)

    hot = ((iota((size, channels), 0) // half) % channels == iota((size, channels), 1)).astype(F32).astype(BF)
    day = lambda n, shape, dim: 2 * (iota(shape, dim) % half) + iota(shape, dim) // (channels * half)

    def widened(l, k, count):
        mixed = (0.5 * mix_ref[l].astype(F32) * time_ref[k, l : l + 1]).astype(BF)
        rows = jnp.dot(hot[:count], mixed, preferred_element_type=F32).astype(BF)
        return lax.dot_general(rows, hot[:count], (((1,), (1,)), ((), ())), preferred_element_type=F32)

    for l in range(layers):
        count = size if l == 0 else size // 2
        gap = day(l, (count, count), 1) - day(l, (count, count), 0)
        value = jnp.zeros((count, count), F32)
        for k in range(3):
            value = jnp.where(gap == (k - 1) * 2**l, widened(l, k, count), value)
        if l == 0:
            first_out[...] = value.astype(BF)
        else:
            rest_out[l - 1] = value.astype(BF)

    spare = jnp.zeros((LANES - layers - 1, channels), F32)
    rows8 = jnp.concatenate([0.5 * mix_bias_ref[...], obs_bias_ref[...], spare], 0)
    high, rest = halves(rows8)
    mid, low = halves(rows8 - high.astype(F32))
    nt = lambda a, b: lax.dot_general(a, b, (((1,), (1,)), ((), ())), preferred_element_type=F32)
    column = nt(hot, high) + (nt(hot, mid) + nt(hot, low))
    bias_out[...] = column

    variables = in_ref.shape[0]
    repeat = (iota((variables, LANES), 1) // days == iota((variables, LANES), 0)).astype(F32).astype(BF)
    in_row = lax.dot_general(
        in_ref[...].astype(F32), repeat.astype(F32), (((0,), (0,)), ((), ())), preferred_element_type=F32
    ).astype(BF)
    wide = jnp.dot(hot, in_row, preferred_element_type=F32)
    same = day(0, (size, LANES), 0) == iota((size, LANES), 1) % days
    in_out[:, :LANES] = jnp.where(same, wide, 0.0).astype(BF)
    same = day(0, (size, days), 0) == iota((size, days), 1)
    b_high, b_low = halves(column[:, layers : layers + 1])
    for at, part in ((LANES, b_high), (LANES + days, b_low)):
        in_out[:, at : at + days] = jnp.where(
            same, jnp.broadcast_to(part.astype(F32), (size, days)), 0.0
        ).astype(BF)
    out_row = nt(jnp.broadcast_to(out_ref[...], (8, channels)), hot)
    same = iota((days, size), 0) == day(0, (days, size), 1)
    out_out[...] = jnp.where(same, jnp.broadcast_to(out_row[0:1], (days, size)), 0.0).astype(BF)

    bands, tiles = lax.axis_size("day"), lax.axis_size("tile")
    band_at, tile_at = lax.axis_index("day"), lax.axis_index("tile")
    cols, rows = width - 2 * HALO, 16
    for b in range(valid_out.shape[0]):
        row, q = place_of(b, width, (1, LANES))
        low_r = jnp.where(band_at == 0, HALO, 0)
        high_r = jnp.where(band_at == bands - 1, rows + HALO, rows + 2 * HALO)
        low_q = jnp.where(tile_at == 0, HALO, 0)
        high_q = jnp.where(tile_at == tiles - 1, cols + HALO, cols + 2 * HALO)
        inside = (row >= low_r) & (row < high_r) & (q >= low_q) & (q < high_q)
        valid_out[b : b + 1] = jnp.where(inside, 1.0, 0.0)


def main_kernel(
    sources,
    out_b_ref,
    *refs,
):
    given, out_ref, x_ref, v_ref, y_ref, bias_ref = refs[:12], refs[12], refs[13], refs[14], refs[15], refs[16]
    held, taps_sem, sem = refs[17:29], refs[29], refs[30]
    names = ("arrived", "land", "left", "right", "own", "banded", "first", "rest", "column", "in", "out", "valid")
    arrived_ref, land_ref, land_left_ref, land_right_ref, own_land_ref = held[:5]
    banded_ref, first_ref, rest_ref, column_ref, in_ref, out_w_ref, valid_ref = held[5:]
    copies = {
        name: pltpu.make_async_copy(a, b, sem.at[i])
        for i, (name, a, b) in enumerate(zip(names, given, held))
        if name != "banded"
    }
    for name in ("arrived", "land", "left", "right", "in", "column", "first", "valid", "rest", "out", "own"):
        copies[name].start()
    fetch = [
        pltpu.make_async_copy(given[5].at[l], banded_ref.at[l], taps_sem.at[l]) for l in range(banded_ref.shape[0])
    ]
    channels = banded_ref.shape[1]
    layers = banded_ref.shape[0]
    width = LANES + 2 * HALO
    rows_in = 24

    lane = iota((LANES, LANES), 1)

    def expand(b):
        row, q = place_of(b, width, (LANES, LANES))
        side = jnp.where(q < HALO, 1, jnp.where(q >= LANES + HALO, 2, 0))
        return jnp.where((24 * side + row == iota((LANES, LANES), 0)) & (row < rows_in), 1.0, 0.0).astype(BF)

    copies["arrived"].wait()
    tail = arrived_ref[:, 96:104, :].astype(F32).reshape(8 * sources, LANES).astype(BF)
    pick_r, pick_c = iota((7 * sources, 8 * sources), 0), iota((7 * sources, 8 * sources), 1)
    pick = ((pick_c // 8 == pick_r % sources) & (pick_c % 8 == pick_r // sources)).astype(F32).astype(BF)
    parts = jnp.dot(pick, tail, preferred_element_type=F32).astype(BF)
    side_rows = [parts[j * sources : (j + 1) * sources] for j in range(6)]
    meta = parts[6 * sources :]
    wanted = (iota((16, LANES), 1) == iota((16, LANES), 0) + 72).astype(F32).astype(BF)
    tag_rows = lax.dot_general(wanted, meta, (((1,), (1,)), ((), ())), preferred_element_type=F32)
    repeat = (iota((sources, 8 * sources), 1) // 8 == iota((sources, 8 * sources), 0)).astype(F32).astype(BF)
    tag_wide = jnp.dot(tag_rows.astype(BF), repeat, preferred_element_type=F32)
    m, k = iota((256, 8 * sources), 0), iota((256, 8 * sources), 1)
    same = m // 32 == k % 8
    day_of = (m % 32 + 1).astype(F32)
    perms = [
        jnp.where(same & (tag_wide[b : b + 1] == day_of), 1.0, 0.0).astype(BF) for b in range(3)
    ]
    day_col = (iota((32, sources), 0) + 1).astype(F32)
    hot = [jnp.where(tag_rows[i : i + 1] == day_col, 1.0, 0.0).astype(BF) for i in range(9)]

    lane32 = iota((32, LANES), 1)
    cover = jnp.zeros((32, LANES), F32)
    for side in range(3):
        for band, (lo, hi) in enumerate(((0, 4), (4, 20), (20, 24))):
            got = jnp.dot(hot[3 * side + band], meta, preferred_element_type=F32)
            here = (lane32 >= 24 * side + lo) & (lane32 < 24 * side + hi)
            cover = jnp.where(here, got, cover)
    cover = cover.astype(BF)

    packed = [[None] * 2 for _ in range(4)]
    for j in range(6):
        band = 0 if j == 0 else (2 if j == 5 else 1)
        left = jnp.dot(hot[3 + band], side_rows[j], preferred_element_type=F32)
        right = jnp.dot(hot[6 + band], side_rows[j], preferred_element_type=F32)
        both = jnp.where(lane32 % 8 < 4, left, right)
        half, start = (32 * j) // LANES, (32 * j) % LANES
        here = (lane32 >= start) & (lane32 < start + 32)
        for v in range(4):
            moved = pltpu.roll(both, (start - 32 * v) % LANES, 1)
            had = packed[v][half]
            packed[v][half] = jnp.where(here, moved, 0.0 if had is None else had)
    edges = [jnp.concatenate([packed[v][h] for v in range(4)], 0) for h in range(2)]

    rolled = []
    pairs = []
    for p in range(0, 12, 2):
        band = 0 if p < 2 else (2 if p >= 10 else 1)
        rows = [
            arrived_ref[:, 8 * i : 8 * i + 8, :].astype(F32).reshape(8 * sources, LANES).astype(BF)
            for i in (p, p + 1)
        ]
        both = jnp.dot(perms[band], jnp.concatenate(rows, 1), preferred_element_type=F32)
        pairs += [both[:, :LANES], both[:, LANES:]]
    for p, got in enumerate(pairs):
        for r2 in range(2):
            row = 2 * p + r2
            rolled.append(pltpu.roll(got[128 * r2 : 128 * r2 + 128], (8 * row + 4) % LANES, 1))
    zero = jnp.zeros((LANES, LANES), F32)

    def flat_block(b):
        now, start = (b, 8 * b + 4) if b <= 15 else ((b - 1, 8 * b - 132) if b >= 17 else (16, 132))
        before = now - 1
        now_v = rolled[now] if now < rows_in else zero
        before_v = rolled[before] if before >= 0 else zero
        edge = edges[0] if b <= 16 else edges[1]
        return jnp.where(lane < start - 8, before_v, jnp.where(lane < start, edge, now_v))

    for name in ("land", "left", "right"):
        copies[name].wait()
    land, land_left, land_right = (
        pltpu.roll(
            jnp.concatenate([ref[...].astype(F32), jnp.zeros((LANES - rows_in, LANES), F32)], 0), 4, 1, stride=8, stride_axis=0
        )
        for ref in (land_ref, land_left_ref, land_right_ref)
    )
    lane1 = iota((1, LANES), 1)

    def land_block(b):
        now, start = (b, 8 * b + 4) if b <= 15 else ((b - 1, 8 * b - 132) if b >= 17 else (16, 132))
        pick = lambda a, r: a[r : r + 1] if 0 <= r < rows_in else jnp.zeros((1, LANES), F32)
        value = jnp.where(lane1 < start - 4, pick(land_right, now - 1), pick(land_left, now))
        value = jnp.where(lane1 < start - 8, pick(land, now - 1), value)
        return jnp.where(lane1 < start, value, pick(land, now))

    copies["in"].wait()
    for copy in fetch:
        copy.start()
    for j in range(13):
        pair = []
        for b in (2 * j, 2 * j + 1):
            keep = jnp.dot(cover, expand(b), preferred_element_type=F32)
            pair.append((jnp.concatenate([flat_block(b), keep, keep], 0) * land_block(b)).astype(BF))
        got = jnp.dot(in_ref[...], jnp.concatenate(pair, 1), preferred_element_type=F32).astype(BF)
        x_ref[2 * j] = got[:, :LANES]
        x_ref[2 * j + 1] = got[:, LANES:]

    for name in ("column", "first", "valid"):
        copies[name].wait()
    for l in range(layers):
        bias_ref[l] = jnp.broadcast_to(column_ref[:, l : l + 1], bias_ref.shape[1:])
    for b in (0, 1, 28, 29):
        v_ref[b] = jnp.zeros(v_ref.shape[1:], BF)

    def mix(l, b):
        both = jnp.concatenate([x_ref[b], x_ref[b + 1]], 1)
        ok = jnp.concatenate([valid_ref[b : b + 1], valid_ref[b + 1 : b + 2]], 1)
        bias = bias_ref[l]
        for p in range(2):
            half = slice(256 * p, 256 * p + 256)
            if l == 0:
                acc = jnp.dot(first_ref[half], both, preferred_element_type=F32)
            else:
                acc = jnp.dot(rest_ref[l - 1], both[half], preferred_element_type=F32)
            h = acc + jnp.concatenate([bias[half], bias[half]], 1)
            v = ((h + h * jnp.tanh(h)) * ok).astype(BF)
            v_ref[b + 2, half] = v[:, :LANES]
            v_ref[b + 3, half] = v[:, LANES:]

    def stencil(l, starts, c):
        groups = [slice(c * 16 + 256 * p, c * 16 + 256 * p + 16) for p in range(2)]
        lhs = jnp.concatenate(
            [
                jnp.concatenate([v_ref[b + i, rows] for i in range(6)], 1)
                for b in starts
                for rows in groups
            ],
            0,
        )
        t = [jnp.zeros((LANES, LANES), BF)] + [banded_ref[l, c, i] for i in range(5)]
        t = t + [t[0]]
        rhs = jnp.concatenate([jnp.concatenate([t[a + 1], t[a]], 1) for a in range(6)], 0)
        acc = jnp.dot(lhs, rhs, preferred_element_type=F32)
        at = 0
        for b in starts:
            for rows in groups:
                for h in range(2):
                    part = acc[at : at + 16, LANES * h : LANES * h + LANES]
                    x_ref[b + h, rows] = (x_ref[b + h, rows].astype(F32) + part).astype(BF)
                at += 16

    for l in range(layers):
        pairs_v, pairs_x = (
            range(low * width // LANES, -(-(rows_in - low) * width // LANES), 2) for low in (l, l + 1)
        )
        if l == 1:
            copies["rest"].wait()
        for b in pairs_v:
            mix(l, b)
        fetch[l].wait()
        for c in range(channels):
            stencil(l, pairs_x, c)

    copies["out"].wait()
    copies["own"].wait()
    for j in range(2, 11):
        got = jnp.dot(
            out_w_ref[...], jnp.concatenate([x_ref[2 * j], x_ref[2 * j + 1]], 1), preferred_element_type=F32
        )
        y_ref[2 * j] = got[:, :LANES]
        y_ref[2 * j + 1] = got[:, LANES:]
    lane_d = iota((32, LANES), 1)
    for r in range(16):
        block, start = divmod((r + HALO) * width + HALO, LANES)
        back = (LANES - start) % LANES
        value = pltpu.roll(y_ref[block], back, 1) if back else y_ref[block]
        if start:
            value = jnp.where(lane_d < LANES - start, value, pltpu.roll(y_ref[block + 1], back, 1))
        out_ref[:, r, :] = (value + out_b_ref[0]) * own_land_ref[r : r + 1].astype(F32)


def local(
    scene_rows,
    granule_list,
    land_mask,
    in_weight,
    obs_bias,
    time_taps,
    mix_weight,
    mix_bias,
    space_taps,
    out_weight,
    out_bias,
):
    bands = lax.axis_size("day")
    tiles = lax.axis_size("tile")
    days_here = granule_list.shape[0]
    days = days_here * bands
    rows, cols = land_mask.shape
    channels, variables = in_weight.shape
    layers = mix_weight.shape[0]
    sources = bands * tiles
    width = cols + 2 * HALO
    slots = scene_rows.shape[3]
    n_block = 26

    notes = jnp.transpose(granule_list.reshape(days_here, bands, 3), (2, 1, 0))
    granules = days_here * bands
    outgoing = pl.pallas_call(
        functools.partial(pack_kernel, tiles, bands, days_here),
        out_shape=jax.ShapeDtypeStruct((sources, 104, cols), BF),
        in_specs=[HBM, SMEM],
        out_specs=VMEM,
        scratch_shapes=[
            pltpu.VMEM((variables, slots, cols), BF),
            pltpu.VMEM((variables, slots + 32, cols), F32),
            pltpu.VMEM((bands, 72, cols), F32),
            pltpu.VMEM((granules, 64, cols), BF),
            pltpu.VMEM((granules, 8, cols), F32),
            pltpu.VMEM(((bands + 2) * (tiles + 2), 8, cols), F32),
            pltpu.SemaphoreType.DMA((variables,)),
        ],
        compiler_params=pltpu.CompilerParams(vmem_limit_bytes=60 * 2**20),
        name="pack",
    )(scene_rows.reshape(variables, slots, cols), notes)

    size = channels * days
    shape = lambda *dims, dtype=BF: jax.ShapeDtypeStruct(dims, dtype)
    land_mask, time_taps, outgoing = lax.optimization_barrier((land_mask, time_taps, outgoing))
    params = (
        jnp.transpose(space_taps, (2, 0, 1)),
        jnp.transpose(time_taps, (2, 0, 1)),
        mix_weight,
        mix_bias,
        in_weight.T,
        obs_bias.reshape(1, channels),
        out_weight.reshape(1, channels),
    )
    made = (
        shape(layers, channels, 5, LANES, LANES),
        shape(size, size),
        shape(layers - 1, size // 2, size // 2),
        shape(size, LANES, dtype=F32),
        shape(size, (variables + 2) * days),
        shape(days, size),
        shape(n_block, LANES, dtype=F32),
    )
    weights = pl.pallas_call(
        functools.partial(weights_kernel, width),
        out_shape=made,
        in_specs=[HBM] * 7,
        out_specs=(HBM,) * 7,
        scratch_shapes=[pltpu.SMEM(params[0].shape, F32)]
        + [pltpu.VMEM(a.shape, a.dtype) for a in params[1:]]
        + [pltpu.VMEM(a.shape, a.dtype) for a in made]
        + [pltpu.SemaphoreType.DMA((8,))],
        compiler_params=pltpu.CompilerParams(vmem_limit_bytes=60 * 2**20),
        cost_estimate=pl.CostEstimate(flops=2 * 10**9, bytes_accessed=24 * 2**20, transcendentals=0),
        name="weights",
    )(*params)
    arrived = lax.all_to_all(outgoing, ("day", "tile"), split_axis=0, concat_axis=0, tiled=True)

    forward = lambda n: [(i, i + 1) for i in range(n - 1)]
    backward = lambda n: [(i + 1, i) for i in range(n - 1)]
    land = land_mask.astype(BF)
    land = jnp.concatenate(
        [
            lax.ppermute(land[rows - HALO :], "day", forward(bands)),
            land,
            lax.ppermute(land[:HALO], "day", backward(bands)),
        ],
        0,
    )
    land_left = lax.ppermute(land, "tile", forward(tiles))
    land_right = lax.ppermute(land, "tile", backward(tiles))

    return pl.pallas_call(
        functools.partial(main_kernel, sources),
        out_shape=jax.ShapeDtypeStruct((days, rows, cols), F32),
        in_specs=[SMEM] + [HBM] * 12,
        out_specs=VMEM,
        scratch_shapes=[
            pltpu.VMEM((n_block, channels * days, LANES), BF),
            pltpu.VMEM((n_block + 4, channels * days, LANES), BF),
            pltpu.VMEM((n_block, days, LANES), F32),
            pltpu.VMEM((layers, size, LANES), F32),
        ]
        + [pltpu.VMEM(a.shape, a.dtype) for a in (arrived, land, land_left, land_right, land_mask)]
        + [pltpu.VMEM(a.shape, a.dtype) for a in made]
        + [pltpu.SemaphoreType.DMA((layers,)), pltpu.SemaphoreType.DMA((12,))],
        compiler_params=pltpu.CompilerParams(vmem_limit_bytes=60 * 2**20),
        name="blocks",
    )(out_bias, arrived, land, land_left, land_right, land_mask, *weights)


def solution(mesh):
    placed = (
        P(None, "day", "tile", None, None),
        P("day", "tile", None, None),
        P("day", "tile"),
        P(),
        P(),
        P(),
        P(),
        P(),
        P(),
        P(),
        P(),
    )
    return jax.shard_map(
        local, mesh=mesh, in_specs=placed, out_specs=P(None, "day", "tile"), check_vma=False
    )
```
